32 devices in a mesh: seq: 8 (over z, y), head: 2 (over x), dp: 2 (over core).
Axes of the slice: x: 2, y: 2, z: 4, core: 2. Of those that a mesh axis runs over, the one named last changes fastest.
Arguments:
- activations: bfloat16 [2, 8192, 1024], P('dp', 'seq'), may hold values from -16 to 16
- project_weight: bfloat16 [1024, 3, 1024], P(None, None, 'head'), may hold values from -0.1875 to 0.1875
- merge_weight: bfloat16 [1024, 1024], P('head'), may hold values from -0.1875 to 0.1875
- cotangent: bfloat16 [2, 8192, 1024], P('dp', 'seq'), may hold values from -6 to 6
Outputs:
- attention_out: bfloat16 [2, 8192, 1024], P('dp', 'seq', 'head')
- grad_activations: bfloat16 [2, 8192, 1024], P('dp', 'seq', 'head')
- grad_project: float32 [1024, 3, 1024], P('seq', None, ('head', 'dp'))
- grad_merge: float32 [1024, 1024], P('head', ('seq', 'dp'))
The draws below stay inside these ranges and needn't reach their ends.
All inputs are finite; a program needn't handle non-finite values.
Results may differ from the reference program's by a relative error of at most 0.0079.
Values may be sent and summed in bfloat16 or wider, within the bound.
A program may use at most 192 MiB of HBM per device.

```python
import math
import jax
import jax.numpy as jnp
from jax import lax

D = 1024
HEADS = 16
DH = 64
BLOCK = 128
POOL = 8
SEQ = 8192
BATCH = 2


def draw_activations(key, part):
    key = jax.random.fold_in(key, 7)
    noise_key, row_key, column_key = jax.random.split(key, 3)
    row_scale = jnp.exp(jax.random.uniform(row_key, (BATCH, SEQ, 1), jnp.float32, math.log(0.3), math.log(3.0)))
    column_scale = jnp.exp(jax.random.uniform(column_key, (1, 1, D), jnp.float32, math.log(0.3), math.log(3.0)))
    noise_part = jax.random.normal(noise_key, (BATCH, SEQ, D), jnp.float32)
    return jnp.clip(noise_part * row_scale * column_scale, -16.0, 16.0).astype(jnp.bfloat16)


def spiked(drawn, key, source, target, shards_of, factor):
    owner, partner = [(jnp.arange(drawn.shape[axis_at]) // (drawn.shape[axis_at] // shards_of)).reshape([-1 if axis == axis_at else 1 for axis in range(drawn.ndim)]) for axis_at in (source, target)]
    chosen = jax.random.permutation(key, shards_of)[partner]
    strong = (owner == chosen) | (owner == (partner + shards_of // 2) % shards_of)
    return jnp.where(strong, factor * drawn, drawn)


def shard_levels(key, extent, cuts, least, largest):
    level, own = 1.0, jax.random.fold_in(key, 6)
    for position, blocks in cuts:
        heights = jnp.exp(jax.random.uniform(jax.random.fold_in(own, position), (blocks,), jnp.float32, least / len(cuts), largest / len(cuts)))
        level = level * jnp.repeat(heights, extent[position] // blocks).reshape([-1 if axis == position else 1 for axis in range(len(extent))])
    return level


def centred(key, dims, scale, reach, cuts=(), dtype=jnp.bfloat16):
    values = jax.random.normal(key, dims, jnp.float32) * scale
    if len(cuts) > 0:
        values = shard_levels(key, dims, cuts, -0.22, 0.18) * values
    return jnp.clip(values, min=-reach, max=reach).astype(dtype)


def noise_with(rng, dims, scale, bound, cuts, heavy, held_as=jnp.bfloat16):
    values = scale * jax.random.normal(rng, dims, jnp.float32)
    if cuts:
        values = values * shard_levels(rng, dims, cuts, -0.22, 0.18)
    return jnp.clip(spiked(values, jax.random.fold_in(rng, 3), *heavy), -bound, bound).astype(held_as)


def setup_inputs(seed: int = 0) -> dict:
    arg_keys = jax.random.split(jax.random.key(seed), 5)
    activations = draw_activations(jax.random.fold_in(arg_keys[4], 71), 0)
    project_weight = centred(arg_keys[1], (D, 3, HEADS * DH), D ** -0.5, 0.1875, ((2, 2),))
    merge_weight = centred(arg_keys[2], (HEADS * DH, D), (HEADS * DH) ** -0.5, 0.1875, ((0, 2),))
    cotangent = noise_with(arg_keys[3], (BATCH, SEQ, D), 1.0, 6.0, ((0, 2), (1, 8)), (1, 2, 8, 2.0))
    return {"activations": activations, "project_weight": project_weight, "merge_weight": merge_weight, "cotangent": cotangent}


EPSILON = 1e-06
HIGHEST = lax.Precision.HIGHEST

def unit_rows(vectors):
    return vectors * lax.rsqrt(lax.optimization_barrier(jnp.mean(vectors * vectors, axis=-1, keepdims=True)) + EPSILON)

def pool_tokens(key_rows, value_rows, window):
    token_count, head_count, head_size = key_rows.shape
    pool_shape = (token_count // window, window, head_count, head_size)
    pooled_keys = key_rows.astype(jnp.float32).reshape(pool_shape).mean(axis=1)
    pooled_values = value_rows.astype(jnp.float32).reshape(pool_shape).sum(axis=1) * (1.0 / math.sqrt(window))
    return (pooled_keys, pooled_values)

def sibling_blocks(pooled, entries, block_count):
    groups = pooled.shape[0] // entries
    trailing = pooled.shape[1:]
    grouped = pooled.reshape((groups // 2, 2, entries) + trailing)[:, ::-1]
    grouped = grouped.reshape((groups, 1, entries) + trailing)
    spread = jnp.broadcast_to(grouped, (groups, block_count // groups, entries) + trailing)
    return spread.reshape((block_count, entries) + trailing)

def block_scores(queries, key_rows, block_len):
    token_count, head_count, head_size = queries.shape
    block_shape = (token_count // block_len, block_len, head_count, head_size)
    scores = jnp.einsum('bqhe,bkhe->bhqk', queries.reshape(block_shape), key_rows.reshape(block_shape), preferred_element_type=jnp.float32)
    return scores * (1.0 / math.sqrt(head_size))

def fine_back(grad_fine, queries, key_rows, block_len):
    token_count, head_count, head_size = queries.shape
    block_shape = (token_count // block_len, block_len, head_count, head_size)
    score_scale = 1.0 / math.sqrt(head_size)
    grad_q = jnp.einsum('bhqk,bkhe->bqhe', grad_fine, key_rows.reshape(block_shape), precision=HIGHEST) * score_scale
    grad_k = jnp.einsum('bhqk,bqhe->bkhe', grad_fine, queries.reshape(block_shape), precision=HIGHEST) * score_scale
    return (grad_q.reshape(token_count, head_count, head_size), grad_k.reshape(token_count, head_count, head_size))

def attend(queries, key_rows, value_rows, fine_scores, block_len, window, rounded):
    token_count, head_count, head_size = queries.shape
    block_count = token_count // block_len
    entries = block_len // window
    coarse_keys = []
    coarse_values = []
    for level_index in range(block_count.bit_length() - 1):
        pooled_keys, pooled_values = pool_tokens(key_rows, value_rows, window << level_index)
        coarse_keys.append(sibling_blocks(pooled_keys, entries, block_count))
        coarse_values.append(sibling_blocks(pooled_values, entries, block_count))
    score_scale = 1.0 / math.sqrt(head_size)
    block_shape = (block_count, block_len, head_count, head_size)
    query_blocks = queries.reshape(block_shape)
    value_blocks = value_rows.reshape(block_shape)
    fine_exp = jnp.exp(fine_scores)
    all_keys = jnp.concatenate(coarse_keys, axis=1)
    all_values = jnp.concatenate(coarse_values, axis=1)
    coarse_scores = jnp.einsum('bqhe,bche->bhqc', query_blocks, all_keys, precision=HIGHEST) * score_scale
    coarse_exp = jnp.exp(coarse_scores)
    denominator = lax.optimization_barrier(jnp.sum(fine_exp, axis=-1)) + lax.optimization_barrier(jnp.sum(coarse_exp, axis=-1))
    inverse = 1.0 / denominator
    fine_weights = fine_exp * inverse[..., None]
    if rounded:
        fine_weights = lax.optimization_barrier(fine_weights.astype(jnp.bfloat16)).astype(jnp.float32)
    combined = jnp.einsum('bhqk,bkhe->bqhe', fine_weights, value_blocks, precision=HIGHEST)
    combined = combined + jnp.einsum('bhqc,bche->bqhe', coarse_exp * inverse[..., None], all_values, precision=HIGHEST)
    return combined.reshape(token_count, head_count, head_size)

def to_heads(array_in):
    return jnp.moveaxis(array_in, 2, 1).reshape(BATCH * HEADS, SEQ, DH)

def from_heads(array_in):
    return jnp.moveaxis(array_in.reshape(BATCH, HEADS, SEQ, DH), 1, 2)

def attention_map(query_arg, key_arg, value_arg, fine_arg):
    return attend(query_arg, key_arg, value_arg, fine_arg, BLOCK, POOL, False)

def per_head(members):
    query_one, key_one, value_one, grad_one = members
    fine_scores = block_scores(query_one[:, None, :], key_one[:, None, :], BLOCK)
    query_full = query_one.astype(jnp.float32)[:, None, :]
    key_full = key_one.astype(jnp.float32)[:, None, :]
    value_full = value_one.astype(jnp.float32)[:, None, :]
    attended = attend(query_full, key_full, value_full, fine_scores, BLOCK, POOL, True)
    _, pull_back = jax.vjp(attention_map, query_full, key_full, value_full, fine_scores)
    grad_q, grad_k, grad_v, grad_fine = pull_back(grad_one.astype(jnp.float32)[:, None, :])
    fine_q, fine_k = fine_back(grad_fine, query_full, key_full, BLOCK)
    grad_q = grad_q + fine_q
    grad_k = grad_k + fine_k
    return (attended[:, 0].astype(jnp.bfloat16), grad_q[:, 0], grad_k[:, 0], grad_v[:, 0])

def reference(activations, project_weight, merge_weight, cotangent):
    total_cols = HEADS * DH
    token_rows = activations.reshape(BATCH * SEQ, D)
    flat_weight = project_weight.reshape(D, 3 * total_cols)
    projected = jnp.dot(token_rows, flat_weight, preferred_element_type=jnp.float32).reshape(BATCH, SEQ, 3, HEADS, DH)
    query_raw = projected[:, :, 0]
    key_raw = projected[:, :, 1]
    value_round = projected[:, :, 2].astype(jnp.bfloat16)
    query_unit = unit_rows(query_raw).astype(jnp.bfloat16)
    key_unit = unit_rows(key_raw).astype(jnp.bfloat16)
    grad_rows = cotangent.reshape(BATCH * SEQ, D)
    grad_attended = jnp.dot(grad_rows, merge_weight.T, preferred_element_type=jnp.float32).astype(jnp.bfloat16)
    grad_attended = grad_attended.reshape(BATCH, SEQ, HEADS, DH)
    results = lax.map(per_head, (to_heads(query_unit), to_heads(key_unit), to_heads(value_round), to_heads(grad_attended)))
    attended = from_heads(results[0]).reshape(BATCH * SEQ, total_cols)
    attention_out = jnp.dot(attended, merge_weight, preferred_element_type=jnp.float32).astype(jnp.bfloat16)
    grad_merge = jnp.dot(attended.T, grad_rows, preferred_element_type=jnp.float32)
    grad_query = from_heads(results[1])
    grad_key = from_heads(results[2])
    grad_value = from_heads(results[3])
    _, query_pull = jax.vjp(unit_rows, query_raw)
    grad_query_raw, = query_pull(grad_query)
    _, key_pull = jax.vjp(unit_rows, key_raw)
    grad_key_raw, = key_pull(grad_key)
    grad_projected = jnp.stack([grad_query_raw, grad_key_raw, grad_value], axis=2).astype(jnp.bfloat16)
    grad_projected = grad_projected.reshape(BATCH * SEQ, 3 * total_cols)
    grad_project = jnp.dot(token_rows.T, grad_projected, preferred_element_type=jnp.float32).reshape(D, 3, total_cols)
    grad_activations = jnp.dot(grad_projected, flat_weight.T, preferred_element_type=jnp.float32).astype(jnp.bfloat16)
    return (attention_out.reshape(BATCH, SEQ, D), grad_activations.reshape(BATCH, SEQ, D), grad_project, grad_merge)
```

```python
import functools
import math

import jax
import jax.numpy as jnp
from jax import lax
from jax.experimental import pallas as pl
from jax.experimental.pallas import tpu as pltpu
from jax.sharding import PartitionSpec as P

DH = 64
BLOCK = 128
POOL = 8
ENTRIES = BLOCK // POOL
LANES = 2 * DH
EPSILON = 1e-06
F32 = jnp.float32
BF16 = jnp.bfloat16
PAIR_FACTORS = (0.5, 1.0 / math.sqrt(2.0))
VMEM_LIMIT = 48 * 1024 * 1024


def dot_nn(a, b):
    return lax.dot_general(a, b, (((1,), (0,)), ((), ())), preferred_element_type=F32)


def dot_nt(a, b):
    return lax.dot_general(a, b, (((1,), (1,)), ((), ())), preferred_element_type=F32)


def dot_tn(a, b):
    return lax.dot_general(a, b, (((0,), (0,)), ((), ())), preferred_element_type=F32)


def low_half(rows):
    return lax.broadcasted_iota(jnp.int32, (rows, LANES), 1) < DH


def half_sums(x, low):
    zero = jnp.zeros_like(x)
    first = jnp.sum(jnp.where(low, x, zero), axis=1, keepdims=True)
    second = jnp.sum(jnp.where(low, zero, x), axis=1, keepdims=True)
    return first, second


def half_means(x, low):
    first, second = half_sums(x, low)
    return jnp.where(low, first, second) * (1.0 / DH)


def pool_matrix(tokens, window):
    entry = lax.broadcasted_iota(jnp.int32, (ENTRIES, tokens), 0)
    token = lax.broadcasted_iota(jnp.int32, (ENTRIES, tokens), 1)
    return (token // window == entry).astype(BF16)


def spread_matrix(tokens, window, offset):
    token = lax.broadcasted_iota(jnp.int32, (tokens, ENTRIES), 0)
    entry = lax.broadcasted_iota(jnp.int32, (tokens, ENTRIES), 1)
    return ((token + offset) // window == entry).astype(BF16)


def project_kernel(act_ref, w_ref, q_ref, k_ref, v_ref, qi_ref, ki_ref, own_ref):
    tokens = act_ref.shape[0]
    width = w_ref.shape[2]
    chunk = min(256, tokens)
    low = low_half(chunk)
    for start in range(0, tokens, chunk):
        rows = pl.ds(start, chunk)
        act = act_ref[rows, :]
        for j, (unit_ref, inv_ref) in enumerate(((q_ref, qi_ref), (k_ref, ki_ref))):
            raw = dot_nn(act, w_ref[j])
            for at in range(0, width, LANES):
                part = raw[:, at : at + LANES]
                inv = lax.rsqrt(half_means(part * part, low) + EPSILON)
                unit_ref[rows, at : at + LANES] = (part * inv).astype(BF16)
                inv_ref[rows, at : at + LANES] = inv
        v_ref[rows, :] = dot_nn(act, w_ref[2]).astype(BF16)
    window = tokens // ENTRIES
    pool = pool_matrix(tokens, window)
    own_ref[0] = dot_nn(pool, k_ref[...]) * (1.0 / window)
    own_ref[1] = dot_nn(pool, v_ref[...]) * (1.0 / math.sqrt(window))


def project(act, weight):
    tokens, model = act.shape
    cols = weight.shape[2]
    width = 256
    col = pl.BlockSpec((tokens, width), lambda i: (0, i))
    return pl.pallas_call(
        project_kernel,
        grid=(cols // width,),
        in_specs=[
            pl.BlockSpec((tokens, model), lambda i: (0, 0)),
            pl.BlockSpec((3, model, width), lambda i: (0, 0, i)),
        ],
        out_specs=[col] * 5 + [pl.BlockSpec((2, ENTRIES, width), lambda i: (0, 0, i))],
        out_shape=[jax.ShapeDtypeStruct((tokens, cols), BF16)] * 3
        + [jax.ShapeDtypeStruct((tokens, cols), F32)] * 2
        + [jax.ShapeDtypeStruct((2, ENTRIES, cols), F32)],
        compiler_params=pltpu.CompilerParams(vmem_limit_bytes=VMEM_LIMIT),
    )(act, weight)


def attend_kernel(
    far_levels, q_ref, k_ref, v_ref, do_ref, qi_ref, far_ref, att_ref, gq_ref, dk_ref, dv_ref, gf_ref
):
    tokens = q_ref.shape[0]
    blocks = tokens // BLOCK
    levels = blocks.bit_length() - 1
    coarse = ENTRIES * (levels + far_levels)
    low = low_half(BLOCK)
    key_scale = [1.0 / (POOL << l) for l in range(levels)]
    value_scale = [1.0 / math.sqrt(POOL << l) for l in range(levels)]
    pooled_k, pooled_v = [], []
    for l in range(levels):
        span = BLOCK << l
        pool = pool_matrix(span, POOL << l)
        pooled_k.append(
            [
                (dot_nn(pool, k_ref[pl.ds(g * span, span), :]) * key_scale[l])
                for g in range(blocks >> l)
            ]
        )
        pooled_v.append(
            [
                (dot_nn(pool, v_ref[pl.ds(g * span, span), :]) * value_scale[l])
                for g in range(blocks >> l)
            ]
        )
    padding = BLOCK - coarse
    pad = [jnp.zeros((padding, LANES), F32)] if padding else []
    live = (lax.broadcasted_iota(jnp.int32, (BLOCK, BLOCK), 1) < coarse).astype(F32)
    low_b = low.astype(BF16)
    high_b = (1 - low.astype(F32)).astype(BF16)
    grad_k = [[None] * (blocks >> l) for l in range(levels)]
    grad_v = [[None] * (blocks >> l) for l in range(levels)]
    far_k = jnp.zeros((far_levels * ENTRIES, LANES), F32)
    far_v = jnp.zeros((far_levels * ENTRIES, LANES), F32)

    def add(held, l, g, value):
        held[l][g] = value if held[l][g] is None else held[l][g] + value

    for b in range(blocks):
        rows = pl.ds(b * BLOCK, BLOCK)
        unit = q_ref[rows, :]
        q = unit * jnp.asarray(0.125, BF16)
        do = do_ref[rows, :]
        kc = jnp.concatenate(
            [pooled_k[l][(b >> l) ^ 1] for l in range(levels)] + [far_ref[0]] + pad, axis=0
        ).astype(BF16)
        vc = jnp.concatenate(
            [pooled_v[l][(b >> l) ^ 1] for l in range(levels)] + [far_ref[1]] + pad, axis=0
        ).astype(BF16)
        kf, vf = k_ref[rows, :], v_ref[rows, :]
        keys = jnp.concatenate([kf * low_b, kf * high_b, kc * low_b, kc * high_b], axis=0)
        values = jnp.concatenate([vf * low_b, vf * high_b, vc * low_b, vc * high_b], axis=0)
        scores = dot_nt(q, keys)
        e = [jnp.exp(scores[:, i * BLOCK : (i + 1) * BLOCK]) for i in range(4)]
        if padding:
            e[2], e[3] = e[2] * live, e[3] * live
        inv = [1.0 / jnp.sum(e[i] + e[i + 2], axis=1, keepdims=True) for i in range(2)]
        p = [e[i] * inv[i % 2] for i in range(4)]
        pb = jnp.concatenate([part.astype(BF16) for part in p], axis=1)
        out = dot_nn(pb, values)
        att_ref[rows, :] = out.astype(BF16)
        delta = half_sums(out * do.astype(F32), low)
        dp = dot_nt(do, values)
        ds = jnp.concatenate(
            [
                (p[i] * (dp[:, i * BLOCK : (i + 1) * BLOCK] - delta[i % 2])).astype(BF16)
                for i in range(4)
            ],
            axis=1,
        )
        dq = dot_nn(ds, keys) * 0.125
        u = unit.astype(F32)
        gq_ref[rows, :] = (qi_ref[rows, :] * (dq - u * half_means(dq * u, low))).astype(BF16)
        dk = dot_tn(ds, q)
        dv = dot_tn(pb, do)
        dk_ref[rows, :] = jnp.where(low, dk[0:BLOCK], dk[BLOCK : 2 * BLOCK])
        dv_ref[rows, :] = jnp.where(low, dv[0:BLOCK], dv[BLOCK : 2 * BLOCK])
        dkc = jnp.where(low, dk[2 * BLOCK : 3 * BLOCK], dk[3 * BLOCK :])
        dvc = jnp.where(low, dv[2 * BLOCK : 3 * BLOCK], dv[3 * BLOCK :])
        for l in range(levels):
            part = slice(l * ENTRIES, (l + 1) * ENTRIES)
            add(grad_k, l, (b >> l) ^ 1, dkc[part])
            add(grad_v, l, (b >> l) ^ 1, dvc[part])
        far_k = far_k + dkc[levels * ENTRIES : coarse]
        far_v = far_v + dvc[levels * ENTRIES : coarse]
    gf_ref[0] = far_k
    gf_ref[1] = far_v
    for b in range(blocks):
        rows = pl.ds(b * BLOCK, BLOCK)
        spread = jnp.concatenate(
            [spread_matrix(BLOCK, POOL << l, (b % (1 << l)) * BLOCK) for l in range(levels)], axis=1
        )
        held_k = [grad_k[l][b >> l] * key_scale[l] for l in range(levels)]
        held_v = [grad_v[l][b >> l] * value_scale[l] for l in range(levels)]
        held_k = jnp.concatenate(held_k, axis=0).astype(BF16)
        held_v = jnp.concatenate(held_v, axis=0).astype(BF16)
        dk_ref[rows, :] += dot_nn(spread, held_k)
        dv_ref[rows, :] += dot_nn(spread, held_v)


def attend(q, k, v, do, qi, far):
    tokens, cols = q.shape
    far_levels = far.shape[1] // ENTRIES
    col = pl.BlockSpec((tokens, LANES), lambda i: (0, i))
    few = pl.BlockSpec((2, far_levels * ENTRIES, LANES), lambda i: (0, 0, i))
    return pl.pallas_call(
        functools.partial(attend_kernel, far_levels),
        grid=(cols // LANES,),
        in_specs=[col] * 5 + [few],
        out_specs=[col] * 4 + [few],
        out_shape=[jax.ShapeDtypeStruct((tokens, cols), BF16)] * 2
        + [jax.ShapeDtypeStruct((tokens, cols), F32)] * 2
        + [jax.ShapeDtypeStruct(far.shape, F32)],
        compiler_params=pltpu.CompilerParams(vmem_limit_bytes=VMEM_LIMIT),
    )(q, k, v, do, qi, far)


def finish_kernel(k_ref, ki_ref, dk_ref, dv_ref, far_ref, gk_ref, gv_ref):
    tokens = k_ref.shape[0]
    window = tokens // ENTRIES
    far_k = (far_ref[0] * (1.0 / window)).astype(BF16)
    far_v = (far_ref[1] * (1.0 / math.sqrt(window))).astype(BF16)
    chunk = min(256, tokens)
    low = low_half(chunk)
    for start in range(0, tokens, chunk):
        rows = pl.ds(start, chunk)
        spread = spread_matrix(chunk, window, start)
        g = dk_ref[rows, :] + dot_nn(spread, far_k)
        u = k_ref[rows, :].astype(F32)
        gk_ref[rows, :] = (ki_ref[rows, :] * (g - u * half_means(g * u, low))).astype(BF16)
        gv_ref[rows, :] = (dv_ref[rows, :] + dot_nn(spread, far_v)).astype(BF16)


def finish(k, ki, dk, dv, far):
    tokens, cols = k.shape
    col = pl.BlockSpec((tokens, LANES), lambda i: (0, i))
    return pl.pallas_call(
        finish_kernel,
        grid=(cols // LANES,),
        in_specs=[col] * 4 + [pl.BlockSpec((2, ENTRIES, LANES), lambda i: (0, 0, i))],
        out_specs=[col] * 2,
        out_shape=[jax.ShapeDtypeStruct((tokens, cols), BF16)] * 2,
        compiler_params=pltpu.CompilerParams(vmem_limit_bytes=VMEM_LIMIT),
    )(k, ki, dk, dv, far)


def partner_2(value, axis, apart):
    mask = 2**apart
    pairs = [(source, source ^ mask) for source in range(lax.axis_size(axis))]
    return lax.ppermute(value, axis, pairs)


def pair_factors():
    return jnp.array(PAIR_FACTORS, F32)[:, None, None]


def pair_stack(stacked):
    half_count = stacked.shape[1] // 2
    return stacked.reshape(2, half_count, 2, stacked.shape[2]).sum(axis=2) * pair_factors()


def local(activations, project_weight, merge_weight, cotangent):
    act = activations[0]
    cot = cotangent[0]
    tokens, model = act.shape
    cols = project_weight.shape[2]
    weight = jnp.moveaxis(project_weight, 1, 0)
    q, k, v, qi, ki, own = project(act, weight)
    bit_count = lax.axis_size("seq").bit_length() - 1
    seq_index = lax.axis_index("seq")
    uppers = [seq_index >> level & 1 == 1 for level in range(bit_count)]
    received = []
    current = own
    for level in range(bit_count):
        partner = partner_2(current, "seq", level)
        received.append(partner)
        if level + 1 < bit_count:
            lower_half = jnp.where(uppers[level], partner, current)
            upper_half = jnp.where(uppers[level], current, partner)
            current = pair_stack(jnp.concatenate([lower_half, upper_half], axis=1))
    do = dot_nt(cot, merge_weight).astype(BF16)
    att, gq, dk, dv, grad_far = attend(q, k, v, do, qi, jnp.concatenate(received, axis=1))
    partial_out = dot_nn(att, merge_weight).astype(BF16)
    attention_out = lax.psum_scatter(partial_out, "head", scatter_dimension=1, tiled=True)[None]
    out_term = dot_tn(att, cot)
    grad_merge = lax.psum_scatter(out_term, ("seq", "dp"), scatter_dimension=1, tiled=True)
    carried = jnp.zeros_like(own)
    for level in reversed(range(bit_count)):
        spread = jnp.repeat(carried * pair_factors(), 2, axis=1)
        lower_grad, upper_grad = spread[:, :ENTRIES], spread[:, ENTRIES:]
        own_grad = jnp.where(uppers[level], upper_grad, lower_grad)
        partner_grad = jnp.where(uppers[level], lower_grad, upper_grad)
        sent = partner_grad + grad_far[:, level * ENTRIES : (level + 1) * ENTRIES]
        carried = own_grad + partner_2(sent.astype(BF16), "seq", level)
    gk, gv = finish(k, ki, dk, dv, carried)
    grads = jnp.concatenate([gq, gk, gv], axis=1)
    flat = project_weight.reshape(model, 3 * cols)
    input_term = dot_nt(grads, flat).astype(BF16)
    grad_activations = lax.psum_scatter(input_term, "head", scatter_dimension=1, tiled=True)[None]
    data_count = lax.axis_size("dp")
    part_cols = cols // data_count
    shard_count = lax.axis_size("seq")
    shard_rows = model // shard_count
    term = dot_tn(act, grads).reshape(shard_count, shard_rows, 3, data_count, part_cols)
    term = jnp.moveaxis(term, 3, 1).reshape(model * data_count, 3, part_cols)
    grad_project = lax.psum_scatter(term, ("seq", "dp"), scatter_dimension=0, tiled=True)
    return (attention_out, grad_activations, grad_project, grad_merge)


def solution(mesh):
    return jax.shard_map(
        local,
        mesh=mesh,
        in_specs=(
            P("dp", "seq", None),
            P(None, None, "head"),
            P("head", None),
            P("dp", "seq", None),
        ),
        out_specs=(
            P("dp", "seq", "head"),
            P("dp", "seq", "head"),
            P("seq", None, ("head", "dp")),
            P("head", ("seq", "dp")),
        ),
        check_vma=False,
    )
```

```python
import functools
import math

import jax
import jax.numpy as jnp
from jax import lax
from jax.experimental import pallas as pl
from jax.experimental.pallas import tpu as pltpu
from jax.sharding import PartitionSpec as P

DH = 64
BLOCK = 128
POOL = 8
ENTRIES = BLOCK // POOL
LANES = 2 * DH
EPSILON = 1e-06
F32 = jnp.float32
BF16 = jnp.bfloat16
PAIR_FACTORS = (0.5, 1.0 / math.sqrt(2.0))
VMEM_LIMIT = 48 * 1024 * 1024


def dot_nn(a, b):
    return lax.dot_general(a, b, (((1,), (0,)), ((), ())), preferred_element_type=F32)


def dot_nt(a, b):
    return lax.dot_general(a, b, (((1,), (1,)), ((), ())), preferred_element_type=F32)


def dot_tn(a, b):
    return lax.dot_general(a, b, (((0,), (0,)), ((), ())), preferred_element_type=F32)


def low_half(rows):
    return lax.broadcasted_iota(jnp.int32, (rows, LANES), 1) < DH


def half_sums(x, low):
    zero = jnp.zeros_like(x)
    first = jnp.sum(jnp.where(low, x, zero), axis=1, keepdims=True)
    second = jnp.sum(jnp.where(low, zero, x), axis=1, keepdims=True)
    return first, second


def half_means(x, low):
    first, second = half_sums(x, low)
    return jnp.where(low, first, second) * (1.0 / DH)


def pool_matrix(tokens, window):
    entry = lax.broadcasted_iota(jnp.int32, (ENTRIES, tokens), 0)
    token = lax.broadcasted_iota(jnp.int32, (ENTRIES, tokens), 1)
    return (token // window == entry).astype(BF16)


def spread_matrix(tokens, window, offset):
    token = lax.broadcasted_iota(jnp.int32, (tokens, ENTRIES), 0)
    entry = lax.broadcasted_iota(jnp.int32, (tokens, ENTRIES), 1)
    return ((token + offset) // window == entry).astype(BF16)


def project_kernel(act_ref, w_ref, q_ref, k_ref, v_ref, qi_ref, ki_ref, own_ref):
    tokens = act_ref.shape[0]
    width = w_ref.shape[2]
    chunk = min(256, tokens)
    low = low_half(chunk)
    for start in range(0, tokens, chunk):
        rows = pl.ds(start, chunk)
        act = act_ref[rows, :]
        for j, (unit_ref, inv_ref) in enumerate(((q_ref, qi_ref), (k_ref, ki_ref))):
            raw = dot_nn(act, w_ref[j])
            for at in range(0, width, LANES):
                part = raw[:, at : at + LANES]
                inv = lax.rsqrt(half_means(part * part, low) + EPSILON)
                unit_ref[rows, at : at + LANES] = (part * inv).astype(BF16)
                inv_ref[rows, at : at + LANES] = inv
        v_ref[rows, :] = dot_nn(act, w_ref[2]).astype(BF16)
    window = tokens // ENTRIES
    pool = pool_matrix(tokens, window)
    own_ref[0] = dot_nn(pool, k_ref[...]) * (1.0 / window)
    own_ref[1] = dot_nn(pool, v_ref[...]) * (1.0 / math.sqrt(window))


def project(act, weight):
    tokens, model = act.shape
    cols = weight.shape[2]
    width = 256
    col = pl.BlockSpec((tokens, width), lambda i: (0, i))
    return pl.pallas_call(
        project_kernel,
        grid=(cols // width,),
        in_specs=[
            pl.BlockSpec((tokens, model), lambda i: (0, 0)),
            pl.BlockSpec((3, model, width), lambda i: (0, 0, i)),
        ],
        out_specs=[col] * 5 + [pl.BlockSpec((2, ENTRIES, width), lambda i: (0, 0, i))],
        out_shape=[jax.ShapeDtypeStruct((tokens, cols), BF16)] * 3
        + [jax.ShapeDtypeStruct((tokens, cols), F32)] * 2
        + [jax.ShapeDtypeStruct((2, ENTRIES, cols), F32)],
        compiler_params=pltpu.CompilerParams(vmem_limit_bytes=VMEM_LIMIT),
    )(act, weight)


def attend_kernel(
    far_levels, q_ref, k_ref, v_ref, do_ref, qi_ref, far_ref, att_ref, gq_ref, dk_ref, dv_ref, gf_ref
):
    tokens = q_ref.shape[0]
    blocks = tokens // BLOCK
    levels = blocks.bit_length() - 1
    coarse = ENTRIES * (levels + far_levels)
    low = low_half(BLOCK)
    key_scale = [1.0 / (POOL << l) for l in range(levels)]
    value_scale = [1.0 / math.sqrt(POOL << l) for l in range(levels)]
    pooled_k, pooled_v = [], []
    for l in range(levels):
        span = BLOCK << l
        pool = pool_matrix(span, POOL << l)
        pooled_k.append(
            [
                (dot_nn(pool, k_ref[pl.ds(g * span, span), :]) * key_scale[l])
                for g in range(blocks >> l)
            ]
        )
        pooled_v.append(
            [
                (dot_nn(pool, v_ref[pl.ds(g * span, span), :]) * value_scale[l])
                for g in range(blocks >> l)
            ]
        )
    padding = BLOCK - coarse
    pad = [jnp.zeros((padding, LANES), F32)] if padding else []
    live = (lax.broadcasted_iota(jnp.int32, (BLOCK, BLOCK), 1) < coarse).astype(F32)
    low_b = low.astype(BF16)
    high_b = (1 - low.astype(F32)).astype(BF16)
    grad_k = [[None] * (blocks >> l) for l in range(levels)]
    grad_v = [[None] * (blocks >> l) for l in range(levels)]
    far_k = jnp.zeros((far_levels * ENTRIES, LANES), F32)
    far_v = jnp.zeros((far_levels * ENTRIES, LANES), F32)

    def add(held, l, g, value):
        held[l][g] = value if held[l][g] is None else held[l][g] + value

    for b in range(blocks):
        rows = pl.ds(b * BLOCK, BLOCK)
        unit = q_ref[rows, :]
        q = unit * jnp.asarray(0.125, BF16)
        do = do_ref[rows, :]
        kc = jnp.concatenate(
            [pooled_k[l][(b >> l) ^ 1] for l in range(levels)] + [far_ref[0]] + pad, axis=0
        ).astype(BF16)
        vc = jnp.concatenate(
            [pooled_v[l][(b >> l) ^ 1] for l in range(levels)] + [far_ref[1]] + pad, axis=0
        ).astype(BF16)
        kf, vf = k_ref[rows, :], v_ref[rows, :]
        keys = jnp.concatenate([kf * low_b, kf * high_b, kc * low_b, kc * high_b], axis=0)
        values = jnp.concatenate([vf * low_b, vf * high_b, vc * low_b, vc * high_b], axis=0)
        scores = dot_nt(q, keys)
        e = [jnp.exp(scores[:, i * BLOCK : (i + 1) * BLOCK]) for i in range(4)]
        if padding:
            e[2], e[3] = e[2] * live, e[3] * live
        inv = [1.0 / jnp.sum(e[i] + e[i + 2], axis=1, keepdims=True) for i in range(2)]
        p = [e[i] * inv[i % 2] for i in range(4)]
        pb = jnp.concatenate([part.astype(BF16) for part in p], axis=1)
        out = dot_nn(pb, values)
        att_ref[rows, :] = out.astype(BF16)
        delta = half_sums(out * do.astype(F32), low)
        dp = dot_nt(do, values)
        ds = jnp.concatenate(
            [
                (p[i] * (dp[:, i * BLOCK : (i + 1) * BLOCK] - delta[i % 2])).astype(BF16)
                for i in range(4)
            ],
            axis=1,
        )
        dq = dot_nn(ds, keys) * 0.125
        u = unit.astype(F32)
        gq_ref[rows, :] = (qi_ref[rows, :] * (dq - u * half_means(dq * u, low))).astype(BF16)
        dk = dot_tn(ds, q)
        dv = dot_tn(pb, do)
        dk_ref[rows, :] = jnp.where(low, dk[0:BLOCK], dk[BLOCK : 2 * BLOCK])
        dv_ref[rows, :] = jnp.where(low, dv[0:BLOCK], dv[BLOCK : 2 * BLOCK])
        dkc = jnp.where(low, dk[2 * BLOCK : 3 * BLOCK], dk[3 * BLOCK :])
        dvc = jnp.where(low, dv[2 * BLOCK : 3 * BLOCK], dv[3 * BLOCK :])
        for l in range(levels):
            part = slice(l * ENTRIES, (l + 1) * ENTRIES)
            add(grad_k, l, (b >> l) ^ 1, dkc[part])
            add(grad_v, l, (b >> l) ^ 1, dvc[part])
        far_k = far_k + dkc[levels * ENTRIES : coarse]
        far_v = far_v + dvc[levels * ENTRIES : coarse]
    gf_ref[0] = far_k
    gf_ref[1] = far_v
    for b in range(blocks):
        rows = pl.ds(b * BLOCK, BLOCK)
        spread = jnp.concatenate(
            [spread_matrix(BLOCK, POOL << l, (b % (1 << l)) * BLOCK) for l in range(levels)], axis=1
        )
        held_k = [grad_k[l][b >> l] * key_scale[l] for l in range(levels)]
        held_v = [grad_v[l][b >> l] * value_scale[l] for l in range(levels)]
        held_k = jnp.concatenate(held_k, axis=0).astype(BF16)
        held_v = jnp.concatenate(held_v, axis=0).astype(BF16)
        dk_ref[rows, :] += dot_nn(spread, held_k)
        dv_ref[rows, :] += dot_nn(spread, held_v)


def attend(q, k, v, do, qi, far):
    tokens, cols = q.shape
    far_levels = far.shape[1] // ENTRIES
    col = pl.BlockSpec((tokens, LANES), lambda i: (0, i))
    few = pl.BlockSpec((2, far_levels * ENTRIES, LANES), lambda i: (0, 0, i))
    return pl.pallas_call(
        functools.partial(attend_kernel, far_levels),
        grid=(cols // LANES,),
        in_specs=[col] * 5 + [few],
        out_specs=[col] * 4 + [few],
        out_shape=[jax.ShapeDtypeStruct((tokens, cols), BF16)] * 2
        + [jax.ShapeDtypeStruct((tokens, cols), F32)] * 2
        + [jax.ShapeDtypeStruct(far.shape, F32)],
        compiler_params=pltpu.CompilerParams(vmem_limit_bytes=VMEM_LIMIT),
    )(q, k, v, do, qi, far)


def flip(index, group):
    half = index // group
    return half + 1 - 2 * (half % 2)


def collect_kernel(
    act_ref, cot_ref, att_ref, merge_ref, w_ref, gq_ref, k_ref, ki_ref, dk_ref, dv_ref, gf_ref,
    out_ref, gin_ref, gw_ref, gm_ref,
    far_send, far_recv, gk_ref, gv_ref, xs, xr, w_own, w_ds, w_dr, w_ys, w_yr, w_zs, w_zr,
    m_own, m_ds, m_dr, m_ys, m_yr, m_zs, m_zr,
    far_ss, far_rs, x_ss, x_rs, d_ss, d_rs, y_ss, y_rs, z_ss, z_rs,
):
    seq, head, dp = lax.axis_index("seq"), lax.axis_index("head"), lax.axis_index("dp")
    shards = lax.axis_size("seq")
    bits = shards.bit_length() - 1
    tokens, model = act_ref.shape
    cols = att_ref.shape[1]
    half = model // 2
    other = 1 - head
    parity, place = seq % 2, seq // 2
    places = shards // 2
    size = model // shards
    mesh_id = pl.DeviceIdType.MESH
    barrier = pltpu.get_barrier_semaphore()
    peers = [(lax.rem(seq + step, shards), head, dp) for step in range(1, shards)]
    peers += [(seq, other, dp), (seq, head, 1 - dp)]
    for peer in peers:
        pl.semaphore_signal(barrier, inc=1, device_id=peer, device_id_type=mesh_id)
    pl.semaphore_wait(barrier, len(peers))

    def copy(src, dst, send, recv, device):
        return pltpu.make_async_remote_copy(
            src_ref=src, dst_ref=dst, send_sem=send, recv_sem=recv,
            device_id=device, device_id_type=mesh_id,
        )

    started = []
    far_waits = []
    for level in range(bits):
        group = 1 << level
        held = gf_ref[:, level * ENTRIES : (level + 1) * ENTRIES, :]
        held_k = (held[0] * PAIR_FACTORS[0] ** level).astype(BF16)
        held_v = (held[1] * PAIR_FACTORS[1] ** level).astype(BF16)
        for i in range(group):
            slot = group - 1 + i
            row = lax.broadcasted_iota(jnp.int32, (ENTRIES, ENTRIES), 0)
            entry = lax.broadcasted_iota(jnp.int32, (ENTRIES, ENTRIES), 1)
            spread = ((row + ENTRIES * i) // group == entry).astype(BF16)
            far_send[slot, 0] = dot_nn(spread, held_k).astype(BF16)
            far_send[slot, 1] = dot_nn(spread, held_v).astype(BF16)
            there = group - 1 + seq % group
            peer = (flip(seq, group) * group + i, head, dp)
            sent = copy(far_send.at[slot], far_recv.at[there], far_ss.at[slot], far_rs.at[there], peer)
            sent.start()
            started.append(sent)
            far_waits.append(
                copy(far_send.at[slot], far_recv.at[slot], far_ss.at[slot], far_rs.at[slot], peer)
            )

    chunk = 256
    chunks = tokens // chunk
    far_cols = pl.ds(pl.multiple_of(other * half, half), half)
    own_cols = pl.ds(pl.multiple_of(head * half, half), half)

    def send_x(which, r):
        at = which * chunks + r
        sent = copy(xs.at[at], xr.at[at], x_ss.at[at], x_rs.at[at], (seq, other, dp))
        sent.start()
        started.append(sent)
        return sent

    out_copies, in_copies = [], []
    for r in range(chunks):
        xs[r] = dot_nn(att_ref[pl.ds(r * chunk, chunk), :], merge_ref[:, far_cols]).astype(BF16)
        out_copies.append(send_x(0, r))

    def begin_data(c, src, dst):
        sent = copy(src, dst, d_ss.at[c], d_rs.at[c], (seq, head, 1 - dp))
        sent.start()
        started.append(sent)
        return sent

    data_copies, pair_copies, place_copies = {}, {}, {}
    first = dp == 0
    per = max(1, BLOCK // size)

    def merge_term(b, carry):
        lanes = pl.ds(pl.multiple_of(b * BLOCK, BLOCK), BLOCK)
        term = dot_tn(cot_ref[:, lanes], att_ref[...])
        term = term.reshape(per, 2, size // 2, cols)
        m_own[pl.ds(b * per, per)] = jnp.where(first, term[:, 0], term[:, 1])
        m_ds[pl.ds(b * per, per)] = jnp.where(first, term[:, 1], term[:, 0]).astype(BF16)
        return carry

    lax.fori_loop(0, model // BLOCK, merge_term, 0)
    data_copies[3] = begin_data(3, m_ds, m_dr)

    def weight_stage(c, grads):
        width = cols // 2

        def body(b, carry):
            lanes = pl.ds(pl.multiple_of(b * BLOCK, BLOCK), BLOCK)
            term = dot_tn(act_ref[:, lanes], grads[...])
            low_part = term[:, :width].reshape(per, size, width)
            high_part = term[:, width:].reshape(per, size, width)
            w_own[c, pl.ds(b * per, per)] = jnp.where(first, low_part, high_part)
            w_ds[c, pl.ds(b * per, per)] = jnp.where(first, high_part, low_part).astype(BF16)
            return carry

        lax.fori_loop(0, model // BLOCK, body, 0)
        data_copies[c] = begin_data(c, w_ds.at[c], w_dr.at[c])

    def views(c):
        if c == 3:
            return m_own, m_dr, m_ys, m_yr, m_zs, m_zr
        return tuple(ref.at[c] for ref in (w_own, w_dr, w_ys, w_yr, w_zs, w_zr))

    def pair_stage(c):
        own, dr, ys, yr, _, _ = views(c)
        data_copies[c].wait_recv()
        for i in range(places):
            s = 2 * i + 1 - parity
            ys[i] = (own[s] + dr[s].astype(F32)).astype(BF16)
        sent = copy(ys, yr, y_ss.at[c], y_rs.at[c], (seq + 1 - 2 * parity, head, dp))
        sent.start()
        started.append(sent)
        pair_copies[c] = sent

    def place_stage(c):
        own, dr, _, yr, zs, zr = views(c)
        pair_copies[c].wait_recv()
        for step in range(1, places):
            target = (place + step) % places
            s = 2 * target + parity
            zs[step - 1] = (own[s] + dr[s].astype(F32) + yr[target].astype(F32)).astype(BF16)
            sent = copy(
                zs.at[step - 1], zr.at[step - 1], z_ss.at[c, step - 1], z_rs.at[c, step - 1],
                (s, head, dp),
            )
            sent.start()
            started.append(sent)
            place_copies[c, step] = sent

    def final_stage(c):
        own, dr, _, yr, _, zr = views(c)
        total = own[seq] + dr[seq].astype(F32) + yr[place].astype(F32)
        for step in range(1, places):
            place_copies[c, step].wait_recv()
            total = total + zr[step - 1].astype(F32)
        if c == 3:
            gm_ref[...] = total
        else:
            gw_ref[c] = total

    for wait in far_waits:
        wait.wait_recv()
    carried_k = jnp.zeros((ENTRIES, cols), F32)
    carried_v = jnp.zeros((ENTRIES, cols), F32)
    for slot in range(shards - 1):
        carried_k = carried_k + far_recv[slot, 0].astype(F32)
        carried_v = carried_v + far_recv[slot, 1].astype(F32)
    window = tokens // ENTRIES
    carried_k = (carried_k * (1.0 / window)).astype(BF16)
    carried_v = (carried_v * (1.0 / math.sqrt(window))).astype(BF16)
    low = low_half(chunk)
    for r in range(chunks):
        rows = pl.ds(r * chunk, chunk)
        spread = spread_matrix(chunk, window, r * chunk)
        for at in range(0, cols, LANES):
            lanes = slice(at, at + LANES)
            g = dk_ref[rows, lanes] + dot_nn(spread, carried_k[:, lanes])
            u = k_ref[rows, lanes].astype(F32)
            inv = ki_ref[rows, lanes]
            gk_ref[rows, lanes] = (inv * (g - u * half_means(g * u, low))).astype(BF16)
            gv_ref[rows, lanes] = (
                dv_ref[rows, lanes] + dot_nn(spread, carried_v[:, lanes])
            ).astype(BF16)
        total = dot_nt(gq_ref[rows, :], w_ref[0, far_cols, :])
        total = total + dot_nt(gk_ref[rows, :], w_ref[1, far_cols, :])
        total = total + dot_nt(gv_ref[rows, :], w_ref[2, far_cols, :])
        xs[chunks + r] = total.astype(BF16)
        in_copies.append(send_x(1, r))
        if r == 0:
            pair_stage(3)

    def finish_out(r):
        rows = pl.ds(r * chunk, chunk)
        total = dot_nn(att_ref[rows, :], merge_ref[:, own_cols])
        out_copies[r].wait_recv()
        out_ref[rows, :] = (total + xr[r].astype(F32)).astype(BF16)

    def finish_in(r):
        rows = pl.ds(r * chunk, chunk)
        total = dot_nt(gq_ref[rows, :], w_ref[0, own_cols, :])
        total = total + dot_nt(gk_ref[rows, :], w_ref[1, own_cols, :])
        total = total + dot_nt(gv_ref[rows, :], w_ref[2, own_cols, :])
        in_copies[r].wait_recv()
        gin_ref[rows, :] = (total + xr[chunks + r].astype(F32)).astype(BF16)

    weight_stage(0, gq_ref)
    place_stage(3)
    weight_stage(1, gk_ref)
    pair_stage(0)
    weight_stage(2, gv_ref)
    pair_stage(1)
    place_stage(0)
    final_stage(3)
    pair_stage(2)
    place_stage(1)
    for r in range(chunks):
        finish_out(r)
    place_stage(2)
    final_stage(0)
    final_stage(1)
    final_stage(2)
    for r in range(chunks):
        finish_in(r)
    for sent in started:
        sent.wait_send()


def collect(act, cot, att, merge, weight, gq, k, ki, dk, dv, gf, shards):
    tokens, model = act.shape
    cols = att.shape[1]
    size = model // shards
    places = shards // 2
    others = max(1, places - 1)
    chunks = 2 * (tokens // 256)
    width = cols // 2
    vmem = pl.BlockSpec(memory_space=pltpu.VMEM)
    dma = pltpu.SemaphoreType.DMA

    def stages(lead, rows, lanes):
        return [
            pltpu.VMEM(lead + (shards, rows, lanes), F32),
            pltpu.VMEM(lead + (shards, rows, lanes), BF16),
            pltpu.VMEM(lead + (shards, rows, lanes), BF16),
            pltpu.VMEM(lead + (places, rows, lanes), BF16),
            pltpu.VMEM(lead + (places, rows, lanes), BF16),
            pltpu.VMEM(lead + (others, rows, lanes), BF16),
            pltpu.VMEM(lead + (others, rows, lanes), BF16),
        ]

    return pl.pallas_call(
        collect_kernel,
        in_specs=[vmem] * 11,
        out_specs=[vmem] * 4,
        out_shape=[
            jax.ShapeDtypeStruct((tokens, model // 2), BF16),
            jax.ShapeDtypeStruct((tokens, model // 2), BF16),
            jax.ShapeDtypeStruct((3, size, width), F32),
            jax.ShapeDtypeStruct((size // 2, cols), F32),
        ],
        scratch_shapes=[
            pltpu.VMEM((shards - 1, 2, ENTRIES, cols), BF16),
            pltpu.VMEM((shards - 1, 2, ENTRIES, cols), BF16),
            pltpu.VMEM((tokens, cols), BF16),
            pltpu.VMEM((tokens, cols), BF16),
            pltpu.VMEM((chunks, 256, model // 2), BF16),
            pltpu.VMEM((chunks, 256, model // 2), BF16),
        ]
        + stages((3,), size, width)
        + stages((), size // 2, cols)
        + [
            dma((shards - 1,)), dma((shards - 1,)), dma((chunks,)), dma((chunks,)),
            dma((4,)), dma((4,)), dma((4,)), dma((4,)), dma((4, others)), dma((4, others)),
        ],
        compiler_params=pltpu.CompilerParams(
            vmem_limit_bytes=60 * 1024 * 1024, collective_id=1, has_side_effects=True
        ),
    )(act, cot, att, merge, weight, gq, k, ki, dk, dv, gf)


def partner_2(value, axis, apart):
    mask = 2**apart
    pairs = [(source, source ^ mask) for source in range(lax.axis_size(axis))]
    return lax.ppermute(value, axis, pairs)


def pair_factors():
    return jnp.array(PAIR_FACTORS, F32)[:, None, None]


def pair_stack(stacked):
    half_count = stacked.shape[1] // 2
    return stacked.reshape(2, half_count, 2, stacked.shape[2]).sum(axis=2) * pair_factors()


def local(activations, project_weight, merge_weight, cotangent):
    act = activations[0]
    cot = cotangent[0]
    tokens, model = act.shape
    cols = project_weight.shape[2]
    weight = jnp.moveaxis(project_weight, 1, 0)
    q, k, v, qi, ki, own = project(act, weight)
    bit_count = lax.axis_size("seq").bit_length() - 1
    seq_index = lax.axis_index("seq")
    uppers = [seq_index >> level & 1 == 1 for level in range(bit_count)]
    received = []
    current = own
    for level in range(bit_count):
        partner = partner_2(current, "seq", level)
        received.append(partner)
        if level + 1 < bit_count:
            lower_half = jnp.where(uppers[level], partner, current)
            upper_half = jnp.where(uppers[level], current, partner)
            current = pair_stack(jnp.concatenate([lower_half, upper_half], axis=1))
    do = dot_nt(cot, merge_weight).astype(BF16)
    att, gq, dk, dv, grad_far = attend(q, k, v, do, qi, jnp.concatenate(received, axis=1))
    out, grad_in, grad_w, grad_m = collect(
        act, cot, att, merge_weight, weight, gq, k, ki, dk, dv, grad_far, lax.axis_size("seq")
    )
    return (out[None], grad_in[None], jnp.moveaxis(grad_w, 0, 1), grad_m.T)


def solution(mesh):
    return jax.shard_map(
        local,
        mesh=mesh,
        in_specs=(
            P("dp", "seq", None),
            P(None, None, "head"),
            P("head", None),
            P("dp", "seq", None),
        ),
        out_specs=(
            P("dp", "seq", "head"),
            P("dp", "seq", "head"),
            P("seq", None, ("head", "dp")),
            P("head", ("seq", "dp")),
        ),
        check_vma=False,
    )
```

```python
import functools
import math

import jax
import jax.numpy as jnp
from jax import lax
from jax.experimental import pallas as pl
from jax.experimental.pallas import tpu as pltpu
from jax.sharding import PartitionSpec as P

DH = 64
BLOCK = 128
POOL = 8
ENTRIES = BLOCK // POOL
LANES = 2 * DH
EPSILON = 1e-06
F32 = jnp.float32
BF16 = jnp.bfloat16
PAIR_FACTORS = (0.5, 1.0 / math.sqrt(2.0))
VMEM_LIMIT = 48 * 1024 * 1024


def dot_nn(a, b):
    return lax.dot_general(a, b, (((1,), (0,)), ((), ())), preferred_element_type=F32)


def dot_nt(a, b):
    return lax.dot_general(a, b, (((1,), (1,)), ((), ())), preferred_element_type=F32)


def dot_tn(a, b):
    return lax.dot_general(a, b, (((0,), (0,)), ((), ())), preferred_element_type=F32)


def low_half(rows):
    return lax.broadcasted_iota(jnp.int32, (rows, LANES), 1) < DH


def half_sums(x, low):
    zero = jnp.zeros_like(x)
    first = jnp.sum(jnp.where(low, x, zero), axis=1, keepdims=True)
    second = jnp.sum(jnp.where(low, zero, x), axis=1, keepdims=True)
    return first, second


def half_means(x, low):
    first, second = half_sums(x, low)
    return jnp.where(low, first, second) * (1.0 / DH)


def pool_matrix(tokens, window):
    entry = lax.broadcasted_iota(jnp.int32, (ENTRIES, tokens), 0)
    token = lax.broadcasted_iota(jnp.int32, (ENTRIES, tokens), 1)
    return (token // window == entry).astype(BF16)


def spread_matrix(tokens, window, offset):
    token = lax.broadcasted_iota(jnp.int32, (tokens, ENTRIES), 0)
    entry = lax.broadcasted_iota(jnp.int32, (tokens, ENTRIES), 1)
    return ((token + offset) // window == entry).astype(BF16)


def attend_pair(
    far_levels, lanes, q_ref, k_ref, v_ref, do_ref, qi_ref, far_ref, att_ref, gq_ref, dk_ref, dv_ref, gf_ref
):
    tokens = q_ref.shape[0]
    blocks = tokens // BLOCK
    levels = blocks.bit_length() - 1
    coarse = ENTRIES * (levels + far_levels)
    low = low_half(BLOCK)
    key_scale = [1.0 / (POOL << l) for l in range(levels)]
    value_scale = [1.0 / math.sqrt(POOL << l) for l in range(levels)]
    pooled_k, pooled_v = [], []
    for l in range(levels):
        span = BLOCK << l
        pool = pool_matrix(span, POOL << l)
        pooled_k.append(
            [
                (dot_nn(pool, k_ref[pl.ds(g * span, span), lanes]) * key_scale[l])
                for g in range(blocks >> l)
            ]
        )
        pooled_v.append(
            [
                (dot_nn(pool, v_ref[pl.ds(g * span, span), lanes]) * value_scale[l])
                for g in range(blocks >> l)
            ]
        )
    padding = BLOCK - coarse
    pad = [jnp.zeros((padding, LANES), F32)] if padding else []
    live = (lax.broadcasted_iota(jnp.int32, (BLOCK, BLOCK), 1) < coarse).astype(F32)
    low_b = low.astype(BF16)
    high_b = (1 - low.astype(F32)).astype(BF16)
    grad_k = [[None] * (blocks >> l) for l in range(levels)]
    grad_v = [[None] * (blocks >> l) for l in range(levels)]
    far_k = jnp.zeros((far_levels * ENTRIES, LANES), F32)
    far_v = jnp.zeros((far_levels * ENTRIES, LANES), F32)

    def add(held, l, g, value):
        held[l][g] = value if held[l][g] is None else held[l][g] + value

    for b in range(blocks):
        rows = pl.ds(b * BLOCK, BLOCK)
        unit = q_ref[rows, lanes]
        q = unit * jnp.asarray(0.125, BF16)
        do = do_ref[rows, lanes]
        kc = jnp.concatenate(
            [pooled_k[l][(b >> l) ^ 1] for l in range(levels)] + [far_ref[0, :, lanes]] + pad, axis=0
        ).astype(BF16)
        vc = jnp.concatenate(
            [pooled_v[l][(b >> l) ^ 1] for l in range(levels)] + [far_ref[1, :, lanes]] + pad, axis=0
        ).astype(BF16)
        kf, vf = k_ref[rows, lanes], v_ref[rows, lanes]
        keys = jnp.concatenate([kf * low_b, kf * high_b, kc * low_b, kc * high_b], axis=0)
        values = jnp.concatenate([vf * low_b, vf * high_b, vc * low_b, vc * high_b], axis=0)
        scores = dot_nt(q, keys)
        e = [jnp.exp(scores[:, i * BLOCK : (i + 1) * BLOCK]) for i in range(4)]
        if padding:
            e[2], e[3] = e[2] * live, e[3] * live
        inv = [1.0 / jnp.sum(e[i] + e[i + 2], axis=1, keepdims=True) for i in range(2)]
        p = [e[i] * inv[i % 2] for i in range(4)]
        pb = jnp.concatenate([part.astype(BF16) for part in p], axis=1)
        out = dot_nn(pb, values)
        att_ref[rows, lanes] = out.astype(BF16)
        delta = half_sums(out * do.astype(F32), low)
        dp = dot_nt(do, values)
        ds = jnp.concatenate(
            [
                (p[i] * (dp[:, i * BLOCK : (i + 1) * BLOCK] - delta[i % 2])).astype(BF16)
                for i in range(4)
            ],
            axis=1,
        )
        dq = dot_nn(ds, keys) * 0.125
        u = unit.astype(F32)
        gq_ref[rows, lanes] = (qi_ref[rows, lanes] * (dq - u * half_means(dq * u, low))).astype(BF16)
        dk = dot_tn(ds, q)
        dv = dot_tn(pb, do)
        dk_ref[rows, lanes] = jnp.where(low, dk[0:BLOCK], dk[BLOCK : 2 * BLOCK])
        dv_ref[rows, lanes] = jnp.where(low, dv[0:BLOCK], dv[BLOCK : 2 * BLOCK])
        dkc = jnp.where(low, dk[2 * BLOCK : 3 * BLOCK], dk[3 * BLOCK :])
        dvc = jnp.where(low, dv[2 * BLOCK : 3 * BLOCK], dv[3 * BLOCK :])
        for l in range(levels):
            part = slice(l * ENTRIES, (l + 1) * ENTRIES)
            add(grad_k, l, (b >> l) ^ 1, dkc[part])
            add(grad_v, l, (b >> l) ^ 1, dvc[part])
        far_k = far_k + dkc[levels * ENTRIES : coarse]
        far_v = far_v + dvc[levels * ENTRIES : coarse]
    gf_ref[0, :, lanes] = far_k
    gf_ref[1, :, lanes] = far_v
    for b in range(blocks):
        rows = pl.ds(b * BLOCK, BLOCK)
        spread = jnp.concatenate(
            [spread_matrix(BLOCK, POOL << l, (b % (1 << l)) * BLOCK) for l in range(levels)], axis=1
        )
        held_k = [grad_k[l][b >> l] * key_scale[l] for l in range(levels)]
        held_v = [grad_v[l][b >> l] * value_scale[l] for l in range(levels)]
        held_k = jnp.concatenate(held_k, axis=0).astype(BF16)
        held_v = jnp.concatenate(held_v, axis=0).astype(BF16)
        dk_ref[rows, lanes] += dot_nn(spread, held_k)
        dv_ref[rows, lanes] += dot_nn(spread, held_v)


def flip(index, group):
    half = index // group
    return half + 1 - 2 * (half % 2)


def layer_kernel(
    act_ref, cot_ref, merge_ref, w_ref,
    out_ref, gin_ref, gw_ref, gm_ref,
    q_ref, k_ref, v_ref, qi_ref, ki_ref, do_ref, att_ref, gq_ref, dk_ref, dv_ref, gf_ref,
    own_ref, gathered, far_ref, att_other, merge_send, merge_recv,
    far_send, far_recv, gk_ref, gv_ref, xs, xr, w_own, w_ds, w_dr, w_ys, w_yr, w_zs, w_zr,
    m_own, m_ds, m_dr, m_ys, m_yr, m_zs, m_zr,
    own_ss, own_rs, att_ss, att_rs, merge_sem,
    far_ss, far_rs, x_ss, x_rs, d_ss, d_rs, y_ss, y_rs, z_ss, z_rs,
):
    seq, head, dp = lax.axis_index("seq"), lax.axis_index("head"), lax.axis_index("dp")
    shards = lax.axis_size("seq")
    bits = shards.bit_length() - 1
    tokens, model = act_ref.shape
    cols = att_ref.shape[1]
    half = model // 2
    other = 1 - head
    parity, place = seq % 2, seq // 2
    places = shards // 2
    size = model // shards
    mesh_id = pl.DeviceIdType.MESH
    barrier = pltpu.get_barrier_semaphore()
    peers = [(lax.rem(seq + step, shards), head, dp) for step in range(1, shards)]
    peers += [(seq, other, dp), (seq, head, 1 - dp)]
    for peer in peers:
        pl.semaphore_signal(barrier, inc=1, device_id=peer, device_id_type=mesh_id)

    window = tokens // ENTRIES
    chunk = 256
    chunks = tokens // chunk
    low = low_half(chunk)

    def project_rows(r, carry):
        rows = pl.ds(pl.multiple_of(r * chunk, chunk), chunk)
        act = act_ref[rows, :]
        for at in range(0, cols, 256):
            wide = slice(at, at + 256)
            for j, (unit_ref, inv_ref) in enumerate(((q_ref, qi_ref), (k_ref, ki_ref))):
                raw = dot_nn(act, w_ref[j, :, wide])
                for part_at in range(0, 256, LANES):
                    part = raw[:, part_at : part_at + LANES]
                    inv = lax.rsqrt(half_means(part * part, low) + EPSILON)
                    lanes = slice(at + part_at, at + part_at + LANES)
                    unit_ref[rows, lanes] = (part * inv).astype(BF16)
                    inv_ref[rows, lanes] = inv
            v_ref[rows, wide] = dot_nn(act, w_ref[2, :, wide]).astype(BF16)
        return carry

    lax.fori_loop(0, chunks, project_rows, 0)
    pool = pool_matrix(tokens, window)
    own_ref[0] = (dot_nn(pool, k_ref[...]) * (1.0 / window)).astype(BF16)
    own_ref[1] = (dot_nn(pool, v_ref[...]) * (1.0 / math.sqrt(window))).astype(BF16)
    pl.semaphore_wait(barrier, len(peers))

    def copy(src, dst, send, recv, device):
        return pltpu.make_async_remote_copy(
            src_ref=src, dst_ref=dst, send_sem=send, recv_sem=recv,
            device_id=device, device_id_type=mesh_id,
        )

    started = []
    far_waits = []
    far_cols = pl.ds(pl.multiple_of(other * half, half), half)
    own_cols = pl.ds(pl.multiple_of(head * half, half), half)
    own_waits = []
    for step in range(1, shards):
        peer = (lax.rem(seq + step, shards), head, dp)
        sent = copy(own_ref, gathered.at[seq], own_ss.at[step - 1], own_rs.at[step - 1], peer)
        sent.start()
        started.append(sent)
        source = lax.rem(seq + shards - step, shards)
        own_waits.append(
            copy(own_ref, gathered.at[source], own_ss.at[step - 1], own_rs.at[step - 1], peer)
        )
    merge_send[...] = merge_ref[:, far_cols]
    merge_copy = copy(merge_send, merge_recv, merge_sem.at[0], merge_sem.at[1], (seq, other, dp))
    merge_copy.start()
    started.append(merge_copy)

    def attended_back(r, carry):
        rows = pl.ds(pl.multiple_of(r * chunk, chunk), chunk)
        do_ref[rows, :] = dot_nt(cot_ref[rows, :], merge_ref[...]).astype(BF16)
        return carry

    lax.fori_loop(0, chunks, attended_back, 0)
    for wait in own_waits:
        wait.wait_recv()
    for level in range(bits):
        group = 1 << level
        held = gathered[pl.ds(flip(seq, group) * group, group)]
        pool = pool_matrix(group * ENTRIES, group)
        part = pl.ds(level * ENTRIES, ENTRIES)
        for kind in range(2):
            mean = dot_nn(pool, held[:, kind].reshape(group * ENTRIES, cols))
            far_ref[kind, part, :] = mean * PAIR_FACTORS[kind] ** level

    def att_copy(p):
        lanes = pl.ds(pl.multiple_of(p * LANES, LANES), LANES)
        return copy(
            att_ref.at[:, lanes], att_other.at[:, lanes], att_ss.at[p], att_rs.at[p],
            (seq, other, dp),
        )

    def pair_body(p, carry):
        lanes = pl.ds(pl.multiple_of(p * LANES, LANES), LANES)
        attend_pair(
            bits, lanes, q_ref, k_ref, v_ref, do_ref, qi_ref, far_ref,
            att_ref, gq_ref, dk_ref, dv_ref, gf_ref,
        )
        att_copy(p).start()
        return carry

    pairs = cols // LANES
    lax.fori_loop(0, pairs, pair_body, 0)
    for p in range(pairs):
        started.append(att_copy(p))
    for level in range(bits):
        group = 1 << level
        held = gf_ref[:, level * ENTRIES : (level + 1) * ENTRIES, :]
        held_k = (held[0] * PAIR_FACTORS[0] ** level).astype(BF16)
        held_v = (held[1] * PAIR_FACTORS[1] ** level).astype(BF16)
        for i in range(group):
            slot = group - 1 + i
            row = lax.broadcasted_iota(jnp.int32, (ENTRIES, ENTRIES), 0)
            entry = lax.broadcasted_iota(jnp.int32, (ENTRIES, ENTRIES), 1)
            spread = ((row + ENTRIES * i) // group == entry).astype(BF16)
            far_send[slot, 0] = dot_nn(spread, held_k).astype(BF16)
            far_send[slot, 1] = dot_nn(spread, held_v).astype(BF16)
            there = group - 1 + seq % group
            peer = (flip(seq, group) * group + i, head, dp)
            sent = copy(far_send.at[slot], far_recv.at[there], far_ss.at[slot], far_rs.at[there], peer)
            sent.start()
            started.append(sent)
            far_waits.append(
                copy(far_send.at[slot], far_recv.at[slot], far_ss.at[slot], far_rs.at[slot], peer)
            )

    def send_x(at):
        sent = copy(xs.at[at], xr.at[at], x_ss.at[at], x_rs.at[at], (seq, other, dp))
        sent.start()
        started.append(sent)
        return sent

    in_copies = []

    def begin_data(c, src, dst):
        sent = copy(src, dst, d_ss.at[c], d_rs.at[c], (seq, head, 1 - dp))
        sent.start()
        started.append(sent)
        return sent

    data_copies, pair_copies, place_copies = {}, {}, {}
    first = dp == 0
    per = max(1, BLOCK // size)

    def merge_term(b, carry):
        lanes = pl.ds(pl.multiple_of(b * BLOCK, BLOCK), BLOCK)
        term = dot_tn(cot_ref[:, lanes], att_ref[...])
        term = term.reshape(per, 2, size // 2, cols)
        m_own[pl.ds(b * per, per)] = jnp.where(first, term[:, 0], term[:, 1])
        m_ds[pl.ds(b * per, per)] = jnp.where(first, term[:, 1], term[:, 0]).astype(BF16)
        return carry

    lax.fori_loop(0, model // BLOCK, merge_term, 0)
    data_copies[3] = begin_data(3, m_ds, m_dr)

    def weight_stage(c, grads):
        width = cols // 2

        def body(b, carry):
            lanes = pl.ds(pl.multiple_of(b * BLOCK, BLOCK), BLOCK)
            term = dot_tn(act_ref[:, lanes], grads[...])
            low_part = term[:, :width].reshape(per, size, width)
            high_part = term[:, width:].reshape(per, size, width)
            w_own[c, pl.ds(b * per, per)] = jnp.where(first, low_part, high_part)
            w_ds[c, pl.ds(b * per, per)] = jnp.where(first, high_part, low_part).astype(BF16)
            return carry

        lax.fori_loop(0, model // BLOCK, body, 0)
        data_copies[c] = begin_data(c, w_ds.at[c], w_dr.at[c])

    def views(c):
        if c == 3:
            return m_own, m_dr, m_ys, m_yr, m_zs, m_zr
        return tuple(ref.at[c] for ref in (w_own, w_dr, w_ys, w_yr, w_zs, w_zr))

    def pair_stage(c):
        own, dr, ys, yr, _, _ = views(c)
        data_copies[c].wait_recv()
        for i in range(places):
            s = 2 * i + 1 - parity
            ys[i] = (own[s] + dr[s].astype(F32)).astype(BF16)
        sent = copy(ys, yr, y_ss.at[c], y_rs.at[c], (seq + 1 - 2 * parity, head, dp))
        sent.start()
        started.append(sent)
        pair_copies[c] = sent

    def place_stage(c):
        own, dr, _, yr, zs, zr = views(c)
        pair_copies[c].wait_recv()
        for step in range(1, places):
            target = (place + step) % places
            s = 2 * target + parity
            zs[step - 1] = (own[s] + dr[s].astype(F32) + yr[target].astype(F32)).astype(BF16)
            sent = copy(
                zs.at[step - 1], zr.at[step - 1], z_ss.at[c, step - 1], z_rs.at[c, step - 1],
                (s, head, dp),
            )
            sent.start()
            started.append(sent)
            place_copies[c, step] = sent

    def final_stage(c):
        own, dr, _, yr, _, zr = views(c)
        total = own[seq] + dr[seq].astype(F32) + yr[place].astype(F32)
        for step in range(1, places):
            place_copies[c, step].wait_recv()
            total = total + zr[step - 1].astype(F32)
        if c == 3:
            gm_ref[...] = total
        else:
            gw_ref[c] = total

    for wait in far_waits:
        wait.wait_recv()
    carried_k = jnp.zeros((ENTRIES, cols), F32)
    carried_v = jnp.zeros((ENTRIES, cols), F32)
    for slot in range(shards - 1):
        carried_k = carried_k + far_recv[slot, 0].astype(F32)
        carried_v = carried_v + far_recv[slot, 1].astype(F32)
    carried_k = (carried_k * (1.0 / window)).astype(BF16)
    carried_v = (carried_v * (1.0 / math.sqrt(window))).astype(BF16)
    for r in range(chunks):
        rows = pl.ds(r * chunk, chunk)
        spread = spread_matrix(chunk, window, r * chunk)
        for at in range(0, cols, LANES):
            lanes = slice(at, at + LANES)
            g = dk_ref[rows, lanes] + dot_nn(spread, carried_k[:, lanes])
            u = k_ref[rows, lanes].astype(F32)
            inv = ki_ref[rows, lanes]
            gk_ref[rows, lanes] = (inv * (g - u * half_means(g * u, low))).astype(BF16)
            gv_ref[rows, lanes] = (
                dv_ref[rows, lanes] + dot_nn(spread, carried_v[:, lanes])
            ).astype(BF16)
        total = dot_nt(gq_ref[rows, :], w_ref[0, far_cols, :])
        total = total + dot_nt(gk_ref[rows, :], w_ref[1, far_cols, :])
        total = total + dot_nt(gv_ref[rows, :], w_ref[2, far_cols, :])
        xs[r] = total.astype(BF16)
        in_copies.append(send_x(r))
        if r == 0:
            pair_stage(3)

    def finish_out(r):
        rows = pl.ds(r * chunk, chunk)
        total = dot_nn(att_ref[rows, :], merge_ref[:, own_cols])
        total = total + dot_nn(att_other[rows, :], merge_recv[...])
        out_ref[rows, :] = total.astype(BF16)

    def finish_in(r):
        rows = pl.ds(r * chunk, chunk)
        total = dot_nt(gq_ref[rows, :], w_ref[0, own_cols, :])
        total = total + dot_nt(gk_ref[rows, :], w_ref[1, own_cols, :])
        total = total + dot_nt(gv_ref[rows, :], w_ref[2, own_cols, :])
        in_copies[r].wait_recv()
        gin_ref[rows, :] = (total + xr[r].astype(F32)).astype(BF16)

    weight_stage(0, gq_ref)
    place_stage(3)
    weight_stage(1, gk_ref)
    pair_stage(0)
    weight_stage(2, gv_ref)
    pair_stage(1)
    place_stage(0)
    final_stage(3)
    pair_stage(2)
    place_stage(1)
    merge_copy.wait_recv()
    for p in range(pairs):
        att_copy(p).wait_recv()
    for r in range(chunks):
        finish_out(r)
    place_stage(2)
    final_stage(0)
    final_stage(1)
    final_stage(2)
    for r in range(chunks):
        finish_in(r)
    for sent in started:
        sent.wait_send()


def layer(act, cot, merge, weight, shards):
    tokens, model = act.shape
    cols = merge.shape[0]
    far_rows = (shards.bit_length() - 1) * ENTRIES
    pairs = cols // LANES
    full, wide = pltpu.VMEM((tokens, cols), BF16), pltpu.VMEM((tokens, cols), F32)
    size = model // shards
    places = shards // 2
    others = max(1, places - 1)
    chunks = tokens // 256
    width = cols // 2
    vmem = pl.BlockSpec(memory_space=pltpu.VMEM)
    dma = pltpu.SemaphoreType.DMA

    def stages(lead, rows, lanes):
        return [
            pltpu.VMEM(lead + (shards, rows, lanes), F32),
            pltpu.VMEM(lead + (shards, rows, lanes), BF16),
            pltpu.VMEM(lead + (shards, rows, lanes), BF16),
            pltpu.VMEM(lead + (places, rows, lanes), BF16),
            pltpu.VMEM(lead + (places, rows, lanes), BF16),
            pltpu.VMEM(lead + (others, rows, lanes), BF16),
            pltpu.VMEM(lead + (others, rows, lanes), BF16),
        ]

    return pl.pallas_call(
        layer_kernel,
        in_specs=[vmem] * 4,
        out_specs=[vmem] * 4,
        out_shape=[
            jax.ShapeDtypeStruct((tokens, model // 2), BF16),
            jax.ShapeDtypeStruct((tokens, model // 2), BF16),
            jax.ShapeDtypeStruct((3, size, width), F32),
            jax.ShapeDtypeStruct((size // 2, cols), F32),
        ],
        scratch_shapes=[full] * 3 + [wide] * 2 + [full] * 3 + [wide] * 2
        + [
            pltpu.VMEM((2, far_rows, cols), F32),
            pltpu.VMEM((2, ENTRIES, cols), BF16),
            pltpu.VMEM((shards, 2, ENTRIES, cols), BF16),
            pltpu.VMEM((2, far_rows, cols), F32),
            full,
            pltpu.VMEM((cols, model // 2), BF16),
            pltpu.VMEM((cols, model // 2), BF16),
            pltpu.VMEM((shards - 1, 2, ENTRIES, cols), BF16),
            pltpu.VMEM((shards - 1, 2, ENTRIES, cols), BF16),
            pltpu.VMEM((tokens, cols), BF16),
            pltpu.VMEM((tokens, cols), BF16),
            pltpu.VMEM((chunks, 256, model // 2), BF16),
            pltpu.VMEM((chunks, 256, model // 2), BF16),
        ]
        + stages((3,), size, width)
        + stages((), size // 2, cols)
        + [
            dma((shards - 1,)), dma((shards - 1,)), dma((pairs,)), dma((pairs,)), dma((2,)),
            dma((shards - 1,)), dma((shards - 1,)), dma((chunks,)), dma((chunks,)),
            dma((4,)), dma((4,)), dma((4,)), dma((4,)), dma((4, others)), dma((4, others)),
        ],
        compiler_params=pltpu.CompilerParams(
            vmem_limit_bytes=60 * 1024 * 1024, collective_id=1, has_side_effects=True
        ),
    )(act, cot, merge, weight)


def local(activations, project_weight, merge_weight, cotangent):
    weight = jnp.moveaxis(project_weight, 1, 0)
    out, grad_in, grad_w, grad_m = layer(
        activations[0], cotangent[0], merge_weight, weight, lax.axis_size("seq")
    )
    return (out[None], grad_in[None], jnp.moveaxis(grad_w, 0, 1), grad_m.T)


def solution(mesh):
    return jax.shard_map(
        local,
        mesh=mesh,
        in_specs=(
            P("dp", "seq", None),
            P(None, None, "head"),
            P("head", None),
            P("dp", "seq", None),
        ),
        out_specs=(
            P("dp", "seq", "head"),
            P("dp", "seq", "head"),
            P("seq", None, ("head", "dp")),
            P("head", ("seq", "dp")),
        ),
        check_vma=False,
    )
```

```python
import functools
import math

import jax
import jax.numpy as jnp
from jax import lax
from jax.experimental import pallas as pl
from jax.experimental.pallas import tpu as pltpu
from jax.sharding import PartitionSpec as P

DH = 64
BLOCK = 128
POOL = 8
ENTRIES = BLOCK // POOL
LANES = 2 * DH
EPSILON = 1e-06
F32 = jnp.float32
BF16 = jnp.bfloat16
PAIR_FACTORS = (0.5, 1.0 / math.sqrt(2.0))
VMEM_LIMIT = 48 * 1024 * 1024


def dot_nn(a, b):
    return lax.dot_general(a, b, (((1,), (0,)), ((), ())), preferred_element_type=F32)


def dot_nt(a, b):
    return lax.dot_general(a, b, (((1,), (1,)), ((), ())), preferred_element_type=F32)


def dot_tn(a, b):
    return lax.dot_general(a, b, (((0,), (0,)), ((), ())), preferred_element_type=F32)


def low_half(rows):
    return lax.broadcasted_iota(jnp.int32, (rows, LANES), 1) < DH


def half_sums(x, low):
    zero = jnp.zeros_like(x)
    first = jnp.sum(jnp.where(low, x, zero), axis=1, keepdims=True)
    second = jnp.sum(jnp.where(low, zero, x), axis=1, keepdims=True)
    return first, second


def half_means(x, low):
    first, second = half_sums(x, low)
    return jnp.where(low, first, second) * (1.0 / DH)


def pool_matrix(tokens, window):
    entry = lax.broadcasted_iota(jnp.int32, (ENTRIES, tokens), 0)
    token = lax.broadcasted_iota(jnp.int32, (ENTRIES, tokens), 1)
    return (token // window == entry).astype(BF16)


def spread_matrix(tokens, window, offset):
    token = lax.broadcasted_iota(jnp.int32, (tokens, ENTRIES), 0)
    entry = lax.broadcasted_iota(jnp.int32, (tokens, ENTRIES), 1)
    return ((token + offset) // window == entry).astype(BF16)


def attend_pair(
    far_levels, lanes, q_ref, k_ref, v_ref, do_ref, qi_ref, far_ref, att_ref, gq_ref, dk_ref, dv_ref, gf_ref
):
    tokens = q_ref.shape[0]
    blocks = tokens // BLOCK
    levels = blocks.bit_length() - 1
    coarse = ENTRIES * (levels + far_levels)
    low = low_half(BLOCK)
    key_scale = [1.0 / (POOL << l) for l in range(levels)]
    value_scale = [1.0 / math.sqrt(POOL << l) for l in range(levels)]
    pooled_k, pooled_v = [], []
    for l in range(levels):
        span = BLOCK << l
        pool = pool_matrix(span, POOL << l)
        pooled_k.append(
            [
                (dot_nn(pool, k_ref[pl.ds(g * span, span), lanes]) * key_scale[l])
                for g in range(blocks >> l)
            ]
        )
        pooled_v.append(
            [
                (dot_nn(pool, v_ref[pl.ds(g * span, span), lanes]) * value_scale[l])
                for g in range(blocks >> l)
            ]
        )
    padding = BLOCK - coarse
    pad = [jnp.zeros((padding, LANES), F32)] if padding else []
    live = (lax.broadcasted_iota(jnp.int32, (BLOCK, BLOCK), 1) < coarse).astype(F32)
    low_b = low.astype(BF16)
    high_b = (1 - low.astype(F32)).astype(BF16)
    grad_k = [[None] * (blocks >> l) for l in range(levels)]
    grad_v = [[None] * (blocks >> l) for l in range(levels)]
    far_k = jnp.zeros((far_levels * ENTRIES, LANES), F32)
    far_v = jnp.zeros((far_levels * ENTRIES, LANES), F32)

    def add(held, l, g, value):
        held[l][g] = value if held[l][g] is None else held[l][g] + value

    for b in range(blocks):
        rows = pl.ds(b * BLOCK, BLOCK)
        unit = q_ref[rows, lanes]
        q = unit * jnp.asarray(0.125, BF16)
        do = do_ref[rows, lanes]
        kc = jnp.concatenate(
            [pooled_k[l][(b >> l) ^ 1] for l in range(levels)] + [far_ref[0, :, lanes]] + pad, axis=0
        ).astype(BF16)
        vc = jnp.concatenate(
            [pooled_v[l][(b >> l) ^ 1] for l in range(levels)] + [far_ref[1, :, lanes]] + pad, axis=0
        ).astype(BF16)
        kf, vf = k_ref[rows, lanes], v_ref[rows, lanes]
        keys = jnp.concatenate([kf * low_b, kf * high_b, kc * low_b, kc * high_b], axis=0)
        values = jnp.concatenate([vf * low_b, vf * high_b, vc * low_b, vc * high_b], axis=0)
        scores = dot_nt(q, keys)
        e = [jnp.exp(scores[:, i * BLOCK : (i + 1) * BLOCK]) for i in range(4)]
        if padding:
            e[2], e[3] = e[2] * live, e[3] * live
        inv = [1.0 / jnp.sum(e[i] + e[i + 2], axis=1, keepdims=True) for i in range(2)]
        p = [e[i] * inv[i % 2] for i in range(4)]
        pb = jnp.concatenate([part.astype(BF16) for part in p], axis=1)
        out = dot_nn(pb, values)
        att_ref[rows, lanes] = out.astype(BF16)
        delta = half_sums(out * do.astype(F32), low)
        dp = dot_nt(do, values)
        ds = jnp.concatenate(
            [
                (p[i] * (dp[:, i * BLOCK : (i + 1) * BLOCK] - delta[i % 2])).astype(BF16)
                for i in range(4)
            ],
            axis=1,
        )
        dq = dot_nn(ds, keys) * 0.125
        u = unit.astype(F32)
        gq_ref[rows, lanes] = (qi_ref[rows, lanes] * (dq - u * half_means(dq * u, low))).astype(BF16)
        dk = dot_tn(ds, q)
        dv = dot_tn(pb, do)
        dk_ref[rows, lanes] = jnp.where(low, dk[0:BLOCK], dk[BLOCK : 2 * BLOCK])
        dv_ref[rows, lanes] = jnp.where(low, dv[0:BLOCK], dv[BLOCK : 2 * BLOCK])
        dkc = jnp.where(low, dk[2 * BLOCK : 3 * BLOCK], dk[3 * BLOCK :])
        dvc = jnp.where(low, dv[2 * BLOCK : 3 * BLOCK], dv[3 * BLOCK :])
        for l in range(levels):
            part = slice(l * ENTRIES, (l + 1) * ENTRIES)
            add(grad_k, l, (b >> l) ^ 1, dkc[part])
            add(grad_v, l, (b >> l) ^ 1, dvc[part])
        far_k = far_k + dkc[levels * ENTRIES : coarse]
        far_v = far_v + dvc[levels * ENTRIES : coarse]
    gf_ref[0, :, lanes] = far_k
    gf_ref[1, :, lanes] = far_v
    for b in range(blocks):
        rows = pl.ds(b * BLOCK, BLOCK)
        spread = jnp.concatenate(
            [spread_matrix(BLOCK, POOL << l, (b % (1 << l)) * BLOCK) for l in range(levels)], axis=1
        )
        held_k = [grad_k[l][b >> l] * key_scale[l] for l in range(levels)]
        held_v = [grad_v[l][b >> l] * value_scale[l] for l in range(levels)]
        held_k = jnp.concatenate(held_k, axis=0).astype(BF16)
        held_v = jnp.concatenate(held_v, axis=0).astype(BF16)
        dk_ref[rows, lanes] += dot_nn(spread, held_k)
        dv_ref[rows, lanes] += dot_nn(spread, held_v)


def flip(index, group):
    half = index // group
    return half + 1 - 2 * (half % 2)


def layer_kernel(
    act_ref, cot_ref, merge_ref, w_ref,
    out_ref, gin_ref, gw_ref, gm_ref,
    q_ref, k_ref, v_ref, qi_ref, ki_ref, do_ref, att_ref, gq_ref, dk_ref, dv_ref, gf_ref,
    own_ref, gathered, far_ref, att_other, merge_send, merge_recv,
    far_send, far_recv, gk_ref, gv_ref, xs, xr, w_own, w_ds, w_dr, w_ys, w_yr, w_zs, w_zr,
    m_own, m_ds, m_dr, m_ys, m_yr, m_zs, m_zr,
    own_ss, own_rs, att_ss, att_rs, merge_sem,
    far_ss, far_rs, x_ss, x_rs, d_ss, d_rs, y_ss, y_rs, z_ss, z_rs,
):
    seq, head, dp = lax.axis_index("seq"), lax.axis_index("head"), lax.axis_index("dp")
    shards = lax.axis_size("seq")
    bits = shards.bit_length() - 1
    tokens, model = act_ref.shape
    cols = att_ref.shape[1]
    half = model // 2
    other = 1 - head
    parity, place = seq % 2, seq // 2
    places = shards // 2
    size = model // shards
    mesh_id = pl.DeviceIdType.MESH
    barrier = pltpu.get_barrier_semaphore()
    peers = [(lax.rem(seq + step, shards), head, dp) for step in range(1, shards)]
    peers += [(seq, other, dp), (seq, head, 1 - dp)]
    for peer in peers:
        pl.semaphore_signal(barrier, inc=1, device_id=peer, device_id_type=mesh_id)

    window = tokens // ENTRIES
    chunk = 256
    chunks = tokens // chunk
    low = low_half(chunk)

    def project_rows(r, carry):
        rows = pl.ds(pl.multiple_of(r * chunk, chunk), chunk)
        act = act_ref[rows, :]
        for at in range(0, cols, 256):
            wide = slice(at, at + 256)
            for j, (unit_ref, inv_ref) in enumerate(((q_ref, qi_ref), (k_ref, ki_ref))):
                raw = dot_nn(act, w_ref[j, :, wide])
                for part_at in range(0, 256, LANES):
                    part = raw[:, part_at : part_at + LANES]
                    inv = lax.rsqrt(half_means(part * part, low) + EPSILON)
                    lanes = slice(at + part_at, at + part_at + LANES)
                    unit_ref[rows, lanes] = (part * inv).astype(BF16)
                    inv_ref[rows, lanes] = inv
            v_ref[rows, wide] = dot_nn(act, w_ref[2, :, wide]).astype(BF16)
        return carry

    lax.fori_loop(0, chunks, project_rows, 0)
    pool = pool_matrix(tokens, window)
    own_ref[0] = (dot_nn(pool, k_ref[...]) * (1.0 / window)).astype(BF16)
    own_ref[1] = (dot_nn(pool, v_ref[...]) * (1.0 / math.sqrt(window))).astype(BF16)
    pl.semaphore_wait(barrier, len(peers))

    def copy(src, dst, send, recv, device):
        return pltpu.make_async_remote_copy(
            src_ref=src, dst_ref=dst, send_sem=send, recv_sem=recv,
            device_id=device, device_id_type=mesh_id,
        )

    started = []
    far_waits = []
    far_cols = pl.ds(pl.multiple_of(other * half, half), half)
    own_cols = pl.ds(pl.multiple_of(head * half, half), half)
    own_waits = []
    for step in range(1, shards):
        peer = (lax.rem(seq + step, shards), head, dp)
        sent = copy(own_ref, gathered.at[seq], own_ss.at[step - 1], own_rs.at[step - 1], peer)
        sent.start()
        started.append(sent)
        source = lax.rem(seq + shards - step, shards)
        own_waits.append(
            copy(own_ref, gathered.at[source], own_ss.at[step - 1], own_rs.at[step - 1], peer)
        )
    merge_send[...] = merge_ref[:, far_cols]
    merge_copy = copy(merge_send, merge_recv, merge_sem.at[0], merge_sem.at[1], (seq, other, dp))
    merge_copy.start()
    started.append(merge_copy)

    def attended_back(r, carry):
        rows = pl.ds(pl.multiple_of(r * chunk, chunk), chunk)
        do_ref[rows, :] = dot_nt(cot_ref[rows, :], merge_ref[...]).astype(BF16)
        return carry

    lax.fori_loop(0, chunks, attended_back, 0)
    for wait in own_waits:
        wait.wait_recv()
    for level in range(bits):
        group = 1 << level
        held = gathered[pl.ds(flip(seq, group) * group, group)]
        pool = pool_matrix(group * ENTRIES, group)
        part = pl.ds(level * ENTRIES, ENTRIES)
        for kind in range(2):
            mean = dot_nn(pool, held[:, kind].reshape(group * ENTRIES, cols))
            far_ref[kind, part, :] = mean * PAIR_FACTORS[kind] ** level

    def begin_data(c, src, dst):
        sent = copy(src, dst, d_ss.at[c], d_rs.at[c], (seq, head, 1 - dp))
        sent.start()
        started.append(sent)
        return sent

    data_copies, pair_copies, place_copies = {}, {}, {}
    first = dp == 0
    per = max(1, BLOCK // size)

    def merge_stage(part):
        width = cols // 2
        at = slice(part * width, (part + 1) * width)

        def body(b, carry):
            lanes = pl.ds(pl.multiple_of(b * BLOCK, BLOCK), BLOCK)
            term = dot_tn(cot_ref[:, lanes], att_ref[:, at])
            term = term.reshape(per, 2, size // 2, width)
            here = pl.ds(b * per, per)
            m_own[part, here] = jnp.where(first, term[:, 0], term[:, 1])
            m_ds[part, here] = jnp.where(first, term[:, 1], term[:, 0]).astype(BF16)
            return carry

        lax.fori_loop(0, model // BLOCK, body, 0)
        data_copies[3 + part] = begin_data(3 + part, m_ds.at[part], m_dr.at[part])

    def weight_stage(c, grads):
        width = cols // 2

        def body(b, carry):
            lanes = pl.ds(pl.multiple_of(b * BLOCK, BLOCK), BLOCK)
            term = dot_tn(act_ref[:, lanes], grads[...])
            low_part = term[:, :width].reshape(per, size, width)
            high_part = term[:, width:].reshape(per, size, width)
            w_own[c, pl.ds(b * per, per)] = jnp.where(first, low_part, high_part)
            w_ds[c, pl.ds(b * per, per)] = jnp.where(first, high_part, low_part).astype(BF16)
            return carry

        lax.fori_loop(0, model // BLOCK, body, 0)
        data_copies[c] = begin_data(c, w_ds.at[c], w_dr.at[c])

    def views(c):
        if c >= 3:
            return tuple(ref.at[c - 3] for ref in (m_own, m_dr, m_ys, m_yr, m_zs, m_zr))
        return tuple(ref.at[c] for ref in (w_own, w_dr, w_ys, w_yr, w_zs, w_zr))

    def pair_stage(c):
        own, dr, ys, yr, _, _ = views(c)
        data_copies[c].wait_recv()
        for i in range(places):
            s = 2 * i + 1 - parity
            ys[i] = (own[s] + dr[s].astype(F32)).astype(BF16)
        sent = copy(ys, yr, y_ss.at[c], y_rs.at[c], (seq + 1 - 2 * parity, head, dp))
        sent.start()
        started.append(sent)
        pair_copies[c] = sent

    def place_stage(c):
        own, dr, _, yr, zs, zr = views(c)
        pair_copies[c].wait_recv()
        for step in range(1, places):
            target = (place + step) % places
            s = 2 * target + parity
            zs[step - 1] = (own[s] + dr[s].astype(F32) + yr[target].astype(F32)).astype(BF16)
            sent = copy(
                zs.at[step - 1], zr.at[step - 1], z_ss.at[c, step - 1], z_rs.at[c, step - 1],
                (s, head, dp),
            )
            sent.start()
            started.append(sent)
            place_copies[c, step] = sent

    def final_stage(c):
        own, dr, _, yr, _, zr = views(c)
        total = own[seq] + dr[seq].astype(F32) + yr[place].astype(F32)
        for step in range(1, places):
            place_copies[c, step].wait_recv()
            total = total + zr[step - 1].astype(F32)
        if c >= 3:
            gm_ref[:, (c - 3) * (cols // 2) : (c - 2) * (cols // 2)] = total
        else:
            gw_ref[c] = total

    def att_copy(p):
        lanes = pl.ds(pl.multiple_of(p * LANES, LANES), LANES)
        return copy(
            att_ref.at[:, lanes], att_other.at[:, lanes], att_ss.at[p], att_rs.at[p],
            (seq, other, dp),
        )

    def pair_body(p, carry):
        lanes = pl.ds(pl.multiple_of(p * LANES, LANES), LANES)
        attend_pair(
            bits, lanes, q_ref, k_ref, v_ref, do_ref, qi_ref, far_ref,
            att_ref, gq_ref, dk_ref, dv_ref, gf_ref,
        )
        att_copy(p).start()
        return carry

    pairs = cols // LANES
    middle = pairs // 2
    lax.fori_loop(0, middle, pair_body, 0)
    merge_stage(0)
    lax.fori_loop(middle, pairs - 1, pair_body, 0)
    pair_stage(3)
    lax.fori_loop(pairs - 1, pairs, pair_body, 0)
    for p in range(pairs):
        started.append(att_copy(p))
    for level in range(bits):
        group = 1 << level
        held = gf_ref[:, level * ENTRIES : (level + 1) * ENTRIES, :]
        held_k = (held[0] * PAIR_FACTORS[0] ** level).astype(BF16)
        held_v = (held[1] * PAIR_FACTORS[1] ** level).astype(BF16)
        for i in range(group):
            slot = group - 1 + i
            row = lax.broadcasted_iota(jnp.int32, (ENTRIES, ENTRIES), 0)
            entry = lax.broadcasted_iota(jnp.int32, (ENTRIES, ENTRIES), 1)
            spread = ((row + ENTRIES * i) // group == entry).astype(BF16)
            far_send[slot, 0] = dot_nn(spread, held_k).astype(BF16)
            far_send[slot, 1] = dot_nn(spread, held_v).astype(BF16)
            there = group - 1 + seq % group
            peer = (flip(seq, group) * group + i, head, dp)
            sent = copy(far_send.at[slot], far_recv.at[there], far_ss.at[slot], far_rs.at[there], peer)
            sent.start()
            started.append(sent)
            far_waits.append(
                copy(far_send.at[slot], far_recv.at[slot], far_ss.at[slot], far_rs.at[slot], peer)
            )

    def send_x(at):
        sent = copy(xs.at[at], xr.at[at], x_ss.at[at], x_rs.at[at], (seq, other, dp))
        sent.start()
        started.append(sent)
        return sent

    in_copies = []

    merge_stage(1)
    place_stage(3)
    weight_stage(0, gq_ref)
    pair_stage(4)
    for wait in far_waits:
        wait.wait_recv()
    carried_k = jnp.zeros((ENTRIES, cols), F32)
    carried_v = jnp.zeros((ENTRIES, cols), F32)
    for slot in range(shards - 1):
        carried_k = carried_k + far_recv[slot, 0].astype(F32)
        carried_v = carried_v + far_recv[slot, 1].astype(F32)
    carried_k = (carried_k * (1.0 / window)).astype(BF16)
    carried_v = (carried_v * (1.0 / math.sqrt(window))).astype(BF16)
    for r in range(chunks):
        rows = pl.ds(r * chunk, chunk)
        spread = spread_matrix(chunk, window, r * chunk)
        for at in range(0, cols, LANES):
            lanes = slice(at, at + LANES)
            g = dk_ref[rows, lanes] + dot_nn(spread, carried_k[:, lanes])
            u = k_ref[rows, lanes].astype(F32)
            inv = ki_ref[rows, lanes]
            gk_ref[rows, lanes] = (inv * (g - u * half_means(g * u, low))).astype(BF16)
            gv_ref[rows, lanes] = (
                dv_ref[rows, lanes] + dot_nn(spread, carried_v[:, lanes])
            ).astype(BF16)
        total = dot_nt(gq_ref[rows, :], w_ref[0, far_cols, :])
        total = total + dot_nt(gk_ref[rows, :], w_ref[1, far_cols, :])
        total = total + dot_nt(gv_ref[rows, :], w_ref[2, far_cols, :])
        xs[r] = total.astype(BF16)
        in_copies.append(send_x(r))
        if r == 0:
            pair_stage(0)
        if r == 1:
            place_stage(4)

    def finish_out(r):
        rows = pl.ds(r * chunk, chunk)
        total = dot_nn(att_ref[rows, :], merge_ref[:, own_cols])
        total = total + dot_nn(att_other[rows, :], merge_recv[...])
        out_ref[rows, :] = total.astype(BF16)

    def finish_in(r):
        rows = pl.ds(r * chunk, chunk)
        total = dot_nt(gq_ref[rows, :], w_ref[0, own_cols, :])
        total = total + dot_nt(gk_ref[rows, :], w_ref[1, own_cols, :])
        total = total + dot_nt(gv_ref[rows, :], w_ref[2, own_cols, :])
        in_copies[r].wait_recv()
        gin_ref[rows, :] = (total + xr[r].astype(F32)).astype(BF16)

    weight_stage(1, gk_ref)
    pair_stage(1)
    place_stage(0)
    weight_stage(2, gv_ref)
    pair_stage(2)
    final_stage(3)
    final_stage(4)
    merge_copy.wait_recv()
    for p in range(pairs):
        att_copy(p).wait_recv()
    for r in range(chunks):
        finish_out(r)
    place_stage(1)
    final_stage(0)
    place_stage(2)
    final_stage(1)
    for r in range(chunks):
        finish_in(r)
    final_stage(2)
    for sent in started:
        sent.wait_send()


def layer(act, cot, merge, weight, shards):
    tokens, model = act.shape
    cols = merge.shape[0]
    far_rows = (shards.bit_length() - 1) * ENTRIES
    pairs = cols // LANES
    full, wide = pltpu.VMEM((tokens, cols), BF16), pltpu.VMEM((tokens, cols), F32)
    size = model // shards
    places = shards // 2
    others = max(1, places - 1)
    chunks = tokens // 256
    width = cols // 2
    vmem = pl.BlockSpec(memory_space=pltpu.VMEM)
    dma = pltpu.SemaphoreType.DMA

    def stages(lead, rows, lanes):
        return [
            pltpu.VMEM(lead + (shards, rows, lanes), F32),
            pltpu.VMEM(lead + (shards, rows, lanes), BF16),
            pltpu.VMEM(lead + (shards, rows, lanes), BF16),
            pltpu.VMEM(lead + (places, rows, lanes), BF16),
            pltpu.VMEM(lead + (places, rows, lanes), BF16),
            pltpu.VMEM(lead + (others, rows, lanes), BF16),
            pltpu.VMEM(lead + (others, rows, lanes), BF16),
        ]

    return pl.pallas_call(
        layer_kernel,
        in_specs=[vmem] * 4,
        out_specs=[vmem] * 4,
        out_shape=[
            jax.ShapeDtypeStruct((tokens, model // 2), BF16),
            jax.ShapeDtypeStruct((tokens, model // 2), BF16),
            jax.ShapeDtypeStruct((3, size, width), F32),
            jax.ShapeDtypeStruct((size // 2, cols), F32),
        ],
        scratch_shapes=[full] * 3 + [wide] * 2 + [full] * 3 + [wide] * 2
        + [
            pltpu.VMEM((2, far_rows, cols), F32),
            pltpu.VMEM((2, ENTRIES, cols), BF16),
            pltpu.VMEM((shards, 2, ENTRIES, cols), BF16),
            pltpu.VMEM((2, far_rows, cols), F32),
            full,
            pltpu.VMEM((cols, model // 2), BF16),
            pltpu.VMEM((cols, model // 2), BF16),
            pltpu.VMEM((shards - 1, 2, ENTRIES, cols), BF16),
            pltpu.VMEM((shards - 1, 2, ENTRIES, cols), BF16),
            pltpu.VMEM((tokens, cols), BF16),
            pltpu.VMEM((tokens, cols), BF16),
            pltpu.VMEM((chunks, 256, model // 2), BF16),
            pltpu.VMEM((chunks, 256, model // 2), BF16),
        ]
        + stages((3,), size, width)
        + stages((2,), size // 2, width)
        + [
            dma((shards - 1,)), dma((shards - 1,)), dma((pairs,)), dma((pairs,)), dma((2,)),
            dma((shards - 1,)), dma((shards - 1,)), dma((chunks,)), dma((chunks,)),
            dma((5,)), dma((5,)), dma((5,)), dma((5,)), dma((5, others)), dma((5, others)),
        ],
        compiler_params=pltpu.CompilerParams(
            vmem_limit_bytes=60 * 1024 * 1024, collective_id=1, has_side_effects=True
        ),
    )(act, cot, merge, weight)


def local(activations, project_weight, merge_weight, cotangent):
    weight = jnp.moveaxis(project_weight, 1, 0)
    out, grad_in, grad_w, grad_m = layer(
        activations[0], cotangent[0], merge_weight, weight, lax.axis_size("seq")
    )
    return (out[None], grad_in[None], jnp.moveaxis(grad_w, 0, 1), grad_m.T)


def solution(mesh):
    return jax.shard_map(
        local,
        mesh=mesh,
        in_specs=(
            P("dp", "seq", None),
            P(None, None, "head"),
            P("head", None),
            P("dp", "seq", None),
        ),
        out_specs=(
            P("dp", "seq", "head"),
            P("dp", "seq", "head"),
            P("seq", None, ("head", "dp")),
            P("head", ("seq", "dp")),
        ),
        check_vma=False,
    )
```
